128 devices in a mesh: grp: 4 (over y), page: 32 (over x, z, core).
Axes of the slice: x: 4, y: 4, z: 4, core: 2. Of those that a mesh axis runs over, the one named last changes fastest.
Arguments:
- tokens: bfloat16 [32768, 3584], P(('grp', 'page')), may hold values from -40 to 40
- page_lengths: int32 [128, 8], P(('grp', 'page')), may hold values from 1 to 128, 256 in all within a row
- page_group: int32 [1024, 1], P(('grp', 'page')), may hold values from 0 to 3; in each aligned block of 8 rows (0 to 7, 8 to 15, ...) at most 4 rows name the same one
- page_report: int32 [1024], P(('grp', 'page')), may hold values from 0 to 15
- attn_gain: float32 [3584], replicated, may hold values from 0.1 to 1.9
- w_query: bfloat16 [3584, 1792], P('page'), may hold values from -1 to 1
- w_keyval: bfloat16 [3584, 512], P('page'), may hold values from -1 to 1
- w_out: bfloat16 [1792, 3584], P('page'), may hold values from -0.125 to 0.125
- doc_gain: float32 [3584], replicated, may hold values from 0.4 to 3.5
- ffn_gain: float32 [3584], replicated, may hold values from 0.1 to 1.9
- gate_up_weight: bfloat16 [2, 3584, 16384], P(None, None, 'page'), may hold values from -0.09375 to 0.09375
- w_down: bfloat16 [16384, 3584], P('page'), may hold values from -0.046875 to 0.046875
Outputs:
- token_states: bfloat16 [32768, 3584], P(('grp', 'page'))
- page_embeddings: bfloat16 [1024, 3584], P(('grp', 'page'))
The draws below stay inside these ranges and needn't reach their ends.
Inputs may be any that keep to these rules, and one draw needn't show every extreme that they name: `page_lengths`: the 8 lengths of one row sum to 256; some length is exactly 128. `page_group`: of the 8 pages of one device at most 4 name the same group, a bound that some block reaches.
All inputs are finite; a program needn't handle non-finite values.
Results may differ from the reference program's by a relative error of at most 0.018.
Values may be sent and summed in bfloat16 or wider, within the bound.
No kernel may reach another device: no remote copies, remote signals or barrier semaphores. Data moves between devices by JAX's collectives and lax.ppermute only.
A program may use at most 128 MiB of HBM per device.

```python
import math
import jax
import jax.numpy as jnp
import numpy as np
from jax import lax

D = 3584
HD = 128
HEADS = 14
KV_HEADS = 2
FFW = 16384
TOKENS_PER_UNIT = 256
PAGES_DEV = 8
REPORTS = 16
PAGE_MOST = 128
CAP = 4
DOC_HEADS = 28
TOKENS = 32768
PAGES = 1024
N_GRP = 4
DEVICES = 128


def draw_tokens(key, part):
    key = jax.random.fold_in(key, 11)
    jitter_key = jax.random.fold_in(key, 0)
    matrix = jax.random.truncated_normal(jitter_key, -6.0, 6.0, (TOKENS, D), jnp.float32)
    return matrix.astype(jnp.bfloat16)


def draw_w_query(key, part):
    key = jax.random.fold_in(key, 12)
    matrix = jax.random.truncated_normal(key, -6.0, 6.0, (D, HEADS * HD), jnp.float32) / D ** 0.5
    return matrix.astype(jnp.bfloat16)


def draw_w_keyval(key, part):
    key = jax.random.fold_in(key, 13)
    matrix = jax.random.truncated_normal(key, -6.0, 6.0, (D, 2 * KV_HEADS * HD), jnp.float32) / D ** 0.5
    return matrix.astype(jnp.bfloat16)


def draw_doc_gain(key, part):
    key = jax.random.fold_in(key, 14)
    low_key = jax.random.fold_in(key, 0)
    gain_values = jax.random.uniform(low_key, (D,), jnp.float32, 0.4, 1.9)
    return gain_values


def touch_ends(result, own_key, smallest, largest):
    place = [jax.random.randint(jax.random.fold_in(own_key, axis), (), 0, length) for axis, length in enumerate(result.shape)]
    widest = result.shape.index(max(result.shape))
    beside = place[:widest] + [(place[widest] + 1) % result.shape[widest]] + place[widest + 1:]
    return result.at[tuple(place)].set(smallest).at[tuple(beside)].set(largest)


def levels(key, dims, shards, smallest, top_value):
    level = 1.0
    for axis_at, parts in shards:
        heights = jax.random.uniform(jax.random.fold_in(jax.random.fold_in(key, 6), axis_at), (parts,), jnp.float32, smallest / len(shards), top_value / len(shards))
        level = level * jnp.repeat(jnp.exp(heights), dims[axis_at] // parts).reshape((-1,) + (1,) * (len(dims) - 1 - axis_at))
    return level


def rank_table(number_of, slope):
    portions = [(1 << 20) // math.isqrt(rank ** slope) + 1 for rank in range(1, number_of + 1)]
    spread = 1 + sum(portions) // (1 << 30)
    return np.cumsum(np.array([max(1, weight // spread) for weight in portions]))


def ranked(own_key, shape, amount, skew):
    table = rank_table(amount, skew)
    ticket = jax.random.randint(jax.random.fold_in(own_key, 1), shape, 0, int(table[amount - 1]))
    rank = jnp.searchsorted(jnp.asarray(table, jnp.int32), ticket, side="right")
    return jax.random.permutation(jax.random.fold_in(own_key, 2), amount)[rank].astype(jnp.int32)


def length_profile(number_of, total, limit, lean):
    weights = [(1 << 20) // math.isqrt(standing ** lean) + 1 for standing in range(2, number_of + 1)]
    spare, holding = total - limit - (number_of - 1), [1] * (number_of - 1)
    while spare > 0:
        movable = [i for i in range(number_of - 1) if holding[i] < limit]
        whole, budget = sum([weights[i] for i in movable]), spare
        for i in movable:
            more = min(limit - holding[i], max(1, budget * weights[i] // whole), spare)
            holding[i] = holding[i] + more
            spare = spare - more
    return np.array([limit] + holding)


def ragged_sizes(own_key, number_of, total, limit, slope):
    if number_of == 2:
        one = jax.random.randint(own_key, (), max(1, total - limit), min(limit, total - 1) + 1)
        return jnp.stack([one, total - one])
    tallies = jnp.asarray(length_profile(number_of, total, limit, slope), jnp.int32)
    pairs = (number_of - 1) // 2
    giver, sink = tallies[1:1 + 2 * pairs:2], tallies[2:2 + 2 * pairs:2]
    room = jnp.minimum(giver - 1, limit - sink)
    moved = jax.random.randint(jax.random.fold_in(own_key, 1), (pairs,), 0, 1 << 20) % (room + 1)
    tallies = tallies.at[1:1 + 2 * pairs:2].set(giver - moved).at[2:2 + 2 * pairs:2].set(sink + moved)
    return tallies[jax.random.permutation(jax.random.fold_in(own_key, 2), number_of)]


def assign_block(rng, own, number, rows, number_of, top, most, lean):
    order = jax.random.permutation(rng, number_of)
    crowded, usual = portions_of(number_of, rows * top, most, lean, True), portions_of(number_of, rows * top, most, lean, False)
    places = jnp.arange(number_of)

    def named(sizes, rotation):
        used = int((sizes > 0).sum())
        fixed = max(1, used // 4)
        shifted = fixed + (places - fixed + rotation * (used - fixed)) % max(1, number_of - fixed)
        return jnp.zeros((number_of,), jnp.int32).at[order[jnp.where(places < fixed, places, shifted)]].set(jnp.asarray(sizes, jnp.int32))

    sizes = jnp.where(number % 4 == 0, named(crowded, number // 4), named(usual, number - number // 4 - 1))
    mixed = jax.random.permutation(jax.random.fold_in(own, 3), number_of)
    giver, sink = mixed[0:number_of // 2 * 2:2], mixed[1:number_of // 2 * 2:2]
    margin = jnp.minimum(sizes[giver] - 1, most - sizes[sink]) // 2
    margin = jnp.where((giver == order[0]) | (sink == order[0]) | (sizes[sink] == 0), 0, jnp.maximum(margin, 0))
    shifted = jax.random.randint(jax.random.fold_in(own, 4), (number_of // 2,), 0, 1 << 20) % (margin + 1)
    sizes = sizes.at[giver].add(-shifted).at[sink].add(shifted)
    members = jnp.searchsorted(jnp.cumsum(sizes), jnp.arange(rows * top), side="right").astype(jnp.int32)
    table = members.reshape(top, rows).T
    table = table[jax.random.permutation(jax.random.fold_in(own, 1), rows)]
    rotation = jax.random.randint(jax.random.fold_in(own, 2), (rows, 1), 0, top)
    return jnp.take_along_axis(table, (jnp.arange(top)[None, :] + rotation) % top, axis=1)


def portions_of(amount, total, bound, skew, full):
    portions = [(1 << 20) // math.isqrt(rank ** skew) + 1 for rank in range(1, amount + 1)]
    largest = bound if full else min(bound, max(-(-total // amount), total * portions[0] // sum(portions)))
    least = 1 if total - largest >= amount - 1 else 0
    holding, spare = [largest] + [least] * (amount - 1), total - largest - least * (amount - 1)
    while spare > 0:
        movable = [i for i in range(1, amount) if holding[i] < largest] or [i for i in range(1, amount) if holding[i] < bound]
        mass, left = sum([portions[i] for i in movable]), spare
        for i in movable:
            addition = min(bound - holding[i], max(1, left * portions[i] // mass), spare)
            holding[i] = holding[i] + addition
            spare = spare - addition
    return np.array(holding)


def noise(stream_key, shape, deviation, most, cuts=(), held_as=jnp.bfloat16):
    level = levels(stream_key, shape, cuts, -0.22, 0.18) if cuts else 1.0
    values = jax.random.normal(stream_key, shape, jnp.float32) * deviation * level
    return jnp.minimum(jnp.maximum(values, -most), most).astype(held_as)


def setup_inputs(seed: int = 0) -> dict:
    key_list = jax.random.split(jax.random.key(seed), 13)
    tokens = draw_tokens(jax.random.fold_in(key_list[12], 71), 0)
    page_lengths = jax.vmap(lambda own: ragged_sizes(own, PAGES_DEV, TOKENS_PER_UNIT, PAGE_MOST, 2))(jax.random.split(key_list[1], DEVICES)).reshape((DEVICES, PAGES_DEV)).astype(jnp.int32)
    page_group_keys = jax.random.split(jax.random.fold_in(key_list[2], 1), PAGES // PAGES_DEV)
    page_group_turns = jax.random.permutation(jax.random.fold_in(key_list[2], 3), PAGES // PAGES_DEV)
    page_group = jax.vmap(lambda own, number: assign_block(jax.random.fold_in(key_list[2], 2), own, number, PAGES_DEV, N_GRP, 1, CAP, 2))(page_group_keys, page_group_turns).reshape((PAGES, 1))
    page_report = touch_ends(ranked(key_list[3], (PAGES,), REPORTS, 1), jax.random.fold_in(key_list[3], 3), 0, REPORTS - 1).astype(jnp.int32)
    attn_gain = jnp.clip(1.0 + 0.18 * jax.random.normal(key_list[4], (D,), jnp.float32), 0.1, 1.9)
    w_query = draw_w_query(jax.random.fold_in(key_list[12], 71), 0)
    w_keyval = draw_w_keyval(jax.random.fold_in(key_list[12], 71), 0)
    w_out = noise(key_list[7], (HEADS * HD, D), (HEADS * HD) ** -0.5, 0.125, ((0, 32),))
    doc_gain = draw_doc_gain(jax.random.fold_in(key_list[12], 71), 0)
    ffn_gain = jnp.clip(1.0 + 0.18 * jax.random.normal(key_list[9], (D,), jnp.float32), 0.1, 1.9)
    gate_up_weight = noise(key_list[10], (2, D, FFW), D ** -0.5, 0.09375, ((2, 32),))
    w_down = noise(key_list[11], (FFW, D), FFW ** -0.5, 0.046875, ((0, 32),))
    return {"tokens": tokens, "page_lengths": page_lengths, "page_group": page_group, "page_report": page_report, "attn_gain": attn_gain, "w_query": w_query, "w_keyval": w_keyval, "w_out": w_out, "doc_gain": doc_gain, "ffn_gain": ffn_gain, "gate_up_weight": gate_up_weight, "w_down": w_down}


def settle(values):
    return lax.optimization_barrier(values.astype(jnp.bfloat16))

def rms_scale(values, gain):
    wide = values.astype(jnp.float32)
    return wide * lax.rsqrt(lax.optimization_barrier(jnp.mean(wide * wide, axis=-1, keepdims=True)) + 1e-06) * gain

def page_index(lengths, count):
    ends = jnp.cumsum(lengths, dtype=jnp.int32)
    position = jnp.arange(count, dtype=jnp.int32)
    return lax.optimization_barrier(jnp.sum((position[:, None] >= ends[None, :]).astype(jnp.int32), axis=1))

def reference(tokens, page_lengths, page_group, page_report, attn_gain, w_query, w_keyval, w_out, doc_gain, ffn_gain, gate_up_weight, w_down):
    blocks = tokens.reshape(DEVICES, TOKENS_PER_UNIT, D)
    share = HEADS // KV_HEADS

    def one_device(packed):
        block, lengths = packed
        normed = rms_scale(block, attn_gain).astype(jnp.bfloat16)
        query = settle(jnp.dot(normed, w_query, preferred_element_type=jnp.float32)).astype(jnp.float32)
        keyval = settle(jnp.dot(normed, w_keyval, preferred_element_type=jnp.float32)).astype(jnp.float32)
        grouped = query.reshape(TOKENS_PER_UNIT, KV_HEADS, share, HD)
        keys = keyval[:, :KV_HEADS * HD].reshape(TOKENS_PER_UNIT, KV_HEADS, HD)
        values = keyval[:, KV_HEADS * HD:].reshape(TOKENS_PER_UNIT, KV_HEADS, HD)
        segment = page_index(lengths, TOKENS_PER_UNIT)
        scores = jnp.einsum('tgjd,sgd->gjts', grouped, keys) / math.sqrt(HD)
        scores = jnp.where(segment[:, None] == segment[None, :], scores, -1e+30)
        weights = settle(jax.nn.softmax(scores, axis=-1)).astype(jnp.float32)
        attended = jnp.einsum('gjts,sgd->tgjd', weights, values).reshape(TOKENS_PER_UNIT, HEADS * HD).astype(jnp.bfloat16)
        states = (block.astype(jnp.float32) + jnp.dot(attended, w_out, preferred_element_type=jnp.float32)).astype(jnp.bfloat16)
        member = (segment[None, :] == jnp.arange(PAGES_DEV, dtype=jnp.int32)[:, None]).astype(jnp.bfloat16)
        pooled_vectors = jnp.dot(member, states, preferred_element_type=jnp.float32) / lengths[:, None].astype(jnp.float32)
        return (states, pooled_vectors.astype(jnp.bfloat16))
    states, pooled_vectors = lax.map(one_device, (blocks, page_lengths))
    vectors = pooled_vectors.reshape(PAGES, D)
    label = page_group[:, 0] * REPORTS + page_report
    keys_doc = settle(rms_scale(vectors, doc_gain)).astype(jnp.float32).reshape(PAGES, DOC_HEADS, HD)
    scores = jnp.einsum('qhd,khd->hqk', keys_doc, keys_doc) / HD
    scores = jnp.where(label[:, None] == label[None, :], scores, -1e+30)
    weights = settle(jax.nn.softmax(scores, axis=-1)).astype(jnp.float32)
    context = jnp.einsum('hqk,khd->qhd', weights, keys_doc).reshape(PAGES, D)
    doc_states = (vectors.astype(jnp.float32) + context).astype(jnp.bfloat16)
    mixed_in = rms_scale(doc_states, ffn_gain).astype(jnp.bfloat16)
    gate = jnp.dot(mixed_in, gate_up_weight[0], preferred_element_type=jnp.float32)
    up = jnp.dot(mixed_in, gate_up_weight[1], preferred_element_type=jnp.float32)
    hidden = (jax.nn.silu(gate) * up).astype(jnp.bfloat16)
    page_embeddings = (doc_states.astype(jnp.float32) + jnp.dot(hidden, w_down, preferred_element_type=jnp.float32)).astype(jnp.bfloat16)
    return (states.reshape(TOKENS, D), page_embeddings)
```

```python
import functools
import math

import jax
import jax.numpy as jnp
from jax import lax
from jax.experimental import pallas as pl
from jax.experimental.pallas import tpu as pltpu
from jax.sharding import PartitionSpec as P

HD = 128
REPORTS = 16
SIDE = 4
WY = 256
BF = jnp.bfloat16
F32 = jnp.float32
MIB = 1 << 20


def vmem():
    return pl.BlockSpec(memory_space=pltpu.VMEM)


def smem():
    return pl.BlockSpec(memory_space=pltpu.SMEM)


def anym():
    return pl.BlockSpec(memory_space=pl.ANY)


def params(mib):
    return pltpu.CompilerParams(vmem_limit_bytes=mib * MIB)


def chip_perm(step):
    pairs = []
    for x in range(SIDE):
        for z in range(SIDE):
            for c in range(2):
                a, b, d = step(x, z, c)
                pairs.append(((x * SIDE + z) * 2 + c, ((a % SIDE) * SIDE + b % SIDE) * 2 + d))
    return pairs


def swap(v):
    return lax.ppermute(v, "page", chip_perm(lambda x, z, c: (x, z, 1 - c)))


def move_a(v, k):
    return lax.ppermute(
        v, "page", chip_perm(lambda x, z, c: (x + k, z, c) if c == 0 else (x, z + k, c))
    )


def move_b(v, k):
    return lax.ppermute(
        v, "page", chip_perm(lambda x, z, c: (x, z + k, c) if c == 0 else (x + k, z, c))
    )


def move_y(v, k):
    return lax.ppermute(v, "grp", [(i, (i + k) % SIDE) for i in range(SIDE)])


def after(v, *others):
    return lax.optimization_barrier((v,) + others)[0]


def rms_scale(values, gain):
    wide = values.astype(F32)
    return wide * lax.rsqrt(jnp.mean(wide * wide, axis=-1, keepdims=True) + 1e-06) * gain


def page_index(lengths, count):
    ends = jnp.cumsum(lengths, dtype=jnp.int32)
    position = jnp.arange(count, dtype=jnp.int32)
    return jnp.sum((position[:, None] >= ends[None, :]).astype(jnp.int32), axis=1)


def run_copies(copies, sems):
    started = []
    for i, (src, dst) in enumerate(copies):
        copy = pltpu.make_async_copy(src, dst, sems.at[i])
        copy.start()
        started.append(copy)
    return started


def gather_line(first, move):
    one = move(first, 1)
    three = move(first, -1)
    half = first.shape[0] // 2
    two_low = move(one[:half], 1)
    two_high = move(three[half:], -1)
    return one, three, two_low, two_high


def qkv_kernel(order, xo, xt, seg_col, seg_row, t, s1, s3, s2a, s2b, out, w, qkv, sems):
    depth = t.shape[1]
    copies = []
    for k, piece, lo, n in ((0, t, 0, 4), (1, s1, 0, 4), (3, s3, 0, 4), (2, s2a, 0, 2), (2, s2b, 2, 2)):
        for j in range(n):
            q = order[k * SIDE + lo + j]
            rows = pl.ds(pl.multiple_of(q * depth, 16), depth)
            copies.append((piece.at[j], w.at[rows, :]))
    for copy in run_copies(copies, sems):
        copy.wait()
    tokens = xo.shape[0]
    tile = 384

    @pl.loop(0, w.shape[1] // tile)
    def _(n):
        cols = pl.ds(pl.multiple_of(n * tile, 128), tile)
        weight = w[:, cols]
        qkv[pl.ds(0, tokens), cols] = jnp.dot(xo[...], weight, preferred_element_type=F32).astype(BF)
        qkv[pl.ds(tokens, tokens), cols] = jnp.dot(xt[...], weight, preferred_element_type=F32).astype(BF)

    heads = out.shape[1] // HD

    @pl.loop(0, 2)
    def _(b):
        rows = pl.ds(pl.multiple_of(b * tokens, tokens), tokens)
        same = seg_col[rows, :] == seg_row[b]
        keys = qkv[rows, heads * HD : (heads + 1) * HD]
        values = qkv[rows, (heads + 1) * HD : (heads + 2) * HD]
        for h in range(heads):
            query = qkv[rows, h * HD : (h + 1) * HD]
            scores = lax.dot_general(
                query, keys, (((1,), (1,)), ((), ())), preferred_element_type=F32
            ) * (1.0 / math.sqrt(HD))
            scores = jnp.where(same, scores, -1e30)
            top = jnp.max(scores, axis=1, keepdims=True)
            e = jnp.exp(scores - top)
            weights = (e / jnp.sum(e, axis=1, keepdims=True)).astype(BF)
            out[rows, h * HD : (h + 1) * HD] = jnp.dot(
                weights, values, preferred_element_type=F32
            ).astype(BF)


def page_qkv(order, x_own, x_other, seg_col, seg_row, pieces):
    tokens, width = x_own.shape
    cols = pieces[0].shape[2]
    return pl.pallas_call(
        qkv_kernel,
        out_shape=jax.ShapeDtypeStruct((2 * tokens, cols - 2 * HD), BF),
        in_specs=[smem()] + [vmem()] * 4 + [anym()] * 5,
        out_specs=vmem(),
        scratch_shapes=[
            pltpu.VMEM((width, cols), BF),
            pltpu.VMEM((2 * tokens, cols), BF),
            pltpu.SemaphoreType.DMA((16,)),
        ],
        compiler_params=params(40),
        cost_estimate=pl.CostEstimate(
            flops=2 * 2 * tokens * width * cols, bytes_accessed=2 * width * cols, transcendentals=0
        ),
    )(order, x_own, x_other, seg_col, seg_row, *pieces)


def out_kernel(
    order, pos, tok_own, tok_other, att, att_in, member, member_t, inv, inv_t,
    w4, u1, u3, u2a, u2b, rt, r1, r3, r2a, r2b,
    st_own, st_other, pool_own, pool_other, w, full, sems,
):
    depth = w4.shape[2]
    wy = w4.shape[3]
    core = pos[0]
    grp = pos[1]
    copies = []
    for i, piece, lo, n in ((0, w4, 0, 4), (1, u1, 0, 4), (3, u3, 0, 4), (2, u2a, 0, 2), (2, u2b, 2, 2)):
        block = lax.rem(grp + (SIDE - i), SIDE)
        cols = pl.ds(pl.multiple_of(block * wy, 128), wy)
        for k in range(n):
            for j in range(SIDE):
                rows = pl.ds(pl.multiple_of(order[(lo + k) * SIDE + j] * depth, 16), depth)
                copies.append((piece.at[k, j], w.at[rows, cols]))
    wr = rt.shape[2]
    for k, piece, lo, n in ((0, rt, 0, 4), (1, r1, 0, 4), (3, r3, 0, 4), (2, r2a, 0, 2), (2, r2b, 2, 2)):
        for j in range(n):
            rows = pl.ds(pl.multiple_of(order[k * SIDE + lo + j] * depth, 16), depth)
            copies.append((piece.at[j], w.at[rows, pl.ds(SIDE * wy, wr)]))
    started = run_copies(copies, sems)
    tokens = tok_own.shape[0]
    half = att.shape[1]
    mine = pl.ds(pl.multiple_of(core * half, 128), half)
    theirs = pl.ds(pl.multiple_of((1 - core) * half, 128), half)
    full[0:tokens, mine] = att[0:tokens, :]
    full[tokens : 2 * tokens, mine] = att[tokens : 2 * tokens, :]
    full[0:tokens, theirs] = att_in[tokens : 2 * tokens, :]
    full[tokens : 2 * tokens, theirs] = att_in[0:tokens, :]
    for copy in started:
        copy.wait()
    tile = 256
    width = w.shape[1]

    @pl.loop(0, width // tile)
    def _(n):
        cols = pl.ds(pl.multiple_of(n * tile, 128), tile)
        there = pl.ds(pl.multiple_of(core * width + n * tile, 128), tile)
        weight = w[:, cols]
        for rows, tok, st, mem, ratio, pool in (
            (0, tok_own, st_own, member, inv, pool_own),
            (tokens, tok_other, st_other, member_t, inv_t, pool_other),
        ):
            projected = jnp.dot(full[rows : rows + tokens, :], weight, preferred_element_type=F32)
            states = (tok[:, there].astype(F32) + projected).astype(BF)
            st[:, cols] = states
            pool[:, cols] = (
                jnp.dot(mem[...], states, preferred_element_type=F32) / ratio[...]
            ).astype(BF)


def page_out(order, pos, tok_own, tok_other, att, att_in, members, lens, y_pieces, r_pieces):
    tokens = tok_own.shape[0]
    depth = y_pieces[0].shape[2]
    width = SIDE * y_pieces[0].shape[3] + r_pieces[0].shape[2]
    rows = SIDE * SIDE * depth
    pages = members[0].shape[0]
    st = jax.ShapeDtypeStruct((tokens, width), BF)
    pool = jax.ShapeDtypeStruct((pages, width), BF)
    return pl.pallas_call(
        out_kernel,
        out_shape=(st, st, pool, pool),
        in_specs=[smem()] * 2 + [vmem()] * 8 + [anym()] * 10,
        out_specs=(vmem(),) * 4,
        scratch_shapes=[
            pltpu.VMEM((rows, width), BF),
            pltpu.VMEM((2 * tokens, rows), BF),
            pltpu.SemaphoreType.DMA((80,)),
        ],
        compiler_params=params(40),
        cost_estimate=pl.CostEstimate(
            flops=2 * 2 * tokens * width * rows, bytes_accessed=2 * width * rows, transcendentals=0
        ),
    )(order, pos, tok_own, tok_other, att, att_in, *members, *lens, *y_pieces, *r_pieces)


def doc_kernel(pos, rows, label_col, label_row, out):
    count = out.shape[0]
    mine = pl.ds(pl.multiple_of(pos[1] * count, count), count)
    keys = rows[:, HD : 2 * HD]
    query = rows[mine, HD : 2 * HD]
    scores = lax.dot_general(
        query, keys, (((1,), (1,)), ((), ())), preferred_element_type=F32
    ) * (1.0 / HD)
    scores = jnp.where(label_col[...] == label_row[...], scores, -1e30)
    top = jnp.max(scores, axis=1, keepdims=True)
    e = jnp.exp(scores - top)
    weights = (e / jnp.sum(e, axis=1, keepdims=True)).astype(BF)
    context = jnp.dot(weights, keys, preferred_element_type=F32)
    out[...] = (rows[mine, 0:HD].astype(F32) + context).astype(BF)


def doc_attention(pos, rows, label_col, label_row):
    count = label_col.shape[0]
    return pl.pallas_call(
        doc_kernel,
        out_shape=jax.ShapeDtypeStruct((count, HD), BF),
        in_specs=[smem()] + [vmem()] * 3,
        out_specs=vmem(),
        compiler_params=params(24),
    )(pos, rows, label_col, label_row)


def ffn_kernel(
    order, order_t, pos, t, b1, b2, b3, tt, c1, c2, c3, gain, gate_up, down, pick,
    own, other, states, x, mixed, hidden, wgu, wd, acc, sems,
):
    core = pos[0]
    width = gain.shape[1]
    units = hidden.shape[1]
    half = units // 2
    weights = []
    n_sem = 32
    for n in range(2):
        for g in range(2):
            weights.append(
                pltpu.make_async_copy(
                    gate_up.at[g, :, n * half : (n + 1) * half],
                    wgu.at[g, :, n * half : (n + 1) * half],
                    sems.at[n_sem + 2 * n + g],
                )
            )
    down_copy = pltpu.make_async_copy(down, wd, sems.at[n_sem + 4])
    copies = []
    for table, side, pieces in ((order, core, (t, b1, b2, b3)), (order_t, 1 - core, (tt, c1, c2, c3))):
        for k, piece in enumerate(pieces):
            for j in range(SIDE):
                head = table[k * SIDE + j] * 2 + side
                copies.append((piece.at[j], x.at[:, pl.ds(pl.multiple_of(head * HD, HD), HD)]))
    started = run_copies(copies, sems)
    for copy in weights:
        copy.start()
    down_copy.start()
    for copy in started:
        copy.wait()
    chunk = 32

    @pl.loop(0, x.shape[0] // chunk)
    def _(i):
        rows = pl.ds(pl.multiple_of(i * chunk, chunk), chunk)
        wide = x[rows, 0:width].astype(F32)
        scale = lax.rsqrt(jnp.mean(wide * wide, axis=1, keepdims=True) + 1e-06)
        mixed[rows, :] = (wide * scale * gain[...]).astype(BF)

    for n in range(2):
        weights[2 * n].wait()
        weights[2 * n + 1].wait()
        cols = slice(n * half, (n + 1) * half)
        gate = jnp.dot(mixed[...], wgu[0, :, cols], preferred_element_type=F32)
        up = jnp.dot(mixed[...], wgu[1, :, cols], preferred_element_type=F32)
        hidden[:, cols] = (gate * jax.nn.sigmoid(gate) * up).astype(BF)
    down_copy.wait()
    tile = 512
    pages = acc.shape[1]

    @pl.loop(0, width // tile)
    def _(n):
        cols = pl.ds(pl.multiple_of(n * tile, 128), tile)
        part = jnp.dot(hidden[...], wd[:, cols], preferred_element_type=F32)
        acc[...] = part.reshape(acc.shape)
        for k in range(SIDE):
            for j in range(SIDE):
                own[j, k, :, cols] = acc[order[16 + k * SIDE + j] * 2 + core].astype(BF)
                other[j, k, :, cols] = acc[order_t[16 + k * SIDE + j] * 2 + 1 - core].astype(BF)
        states[:, cols] = jnp.dot(pick[...], x[:, cols], preferred_element_type=F32)


def feed_forward(order, order_t, pos, pieces, pieces_t, gain, gate_up, down, pick):
    width = gain.shape[1]
    units = down.shape[0]
    pages, count = pick.shape
    part = jax.ShapeDtypeStruct((SIDE, SIDE, pages, width), BF)
    return pl.pallas_call(
        ffn_kernel,
        out_shape=(part, part, jax.ShapeDtypeStruct((pages, width), F32)),
        in_specs=[smem()] * 3 + [anym()] * 8 + [vmem()] + [anym()] * 2 + [vmem()],
        out_specs=(vmem(),) * 3,
        scratch_shapes=[
            pltpu.VMEM((count, 2 * SIDE * SIDE * HD), BF),
            pltpu.VMEM((count, width), BF),
            pltpu.VMEM((count, units), BF),
            pltpu.VMEM((2, width, units), BF),
            pltpu.VMEM((units, width), BF),
            pltpu.VMEM((count // pages, pages, 512), F32),
            pltpu.SemaphoreType.DMA((40,)),
        ],
        compiler_params=params(40),
        cost_estimate=pl.CostEstimate(
            flops=6 * count * width * units, bytes_accessed=6 * width * units, transcendentals=0
        ),
    )(order, order_t, pos, *pieces, *pieces_t, gain, gate_up, down, pick)


def on_device(
    tokens,
    page_lengths,
    page_group,
    page_report,
    attn_gain,
    w_query,
    w_keyval,
    w_out,
    doc_gain,
    ffn_gain,
    gate_up_weight,
    w_down,
):
    count, width = tokens.shape
    pages = page_lengths.shape[1]
    grp = lax.axis_index("grp")
    page = lax.axis_index("page")
    core = page % 2
    z = (page // 2) % SIDE
    x = page // (2 * SIDE)
    pos = jnp.stack([core, grp]).astype(jnp.int32)
    step = jnp.arange(SIDE, dtype=jnp.int32)
    zero_order = (((x - step) % SIDE)[None, :] * SIDE + ((z - step) % SIDE)[:, None]).reshape(-1)
    one_order = (((x - step) % SIDE)[:, None] * SIDE + ((z - step) % SIDE)[None, :]).reshape(-1)
    order = jnp.where(core == 0, zero_order, one_order)
    order_t = jnp.where(core == 0, one_order, zero_order)
    zero_dest = (((x + step) % SIDE)[None, :] * SIDE + ((z + step) % SIDE)[:, None]).reshape(-1)
    one_dest = (((x + step) % SIDE)[:, None] * SIDE + ((z + step) % SIDE)[None, :]).reshape(-1)
    dest = jnp.where(core == 0, zero_dest, one_dest)
    dest_t = jnp.where(core == 0, one_dest, zero_dest)

    out_half = w_out.shape[1] // 2
    q_half = w_query.shape[1] // 2

    def out_cols(c):
        return lax.dynamic_slice_in_dim(w_out, c * out_half, out_half, 1)

    def qkv_cols(c):
        return jnp.concatenate(
            [
                lax.dynamic_slice_in_dim(w_query, c * q_half, q_half, 1),
                lax.dynamic_slice_in_dim(w_keyval, c * HD, HD, 1),
                lax.dynamic_slice_in_dim(w_keyval, (2 + c) * HD, HD, 1),
            ],
            axis=1,
        )

    def pair_up(mine, got):
        low = jnp.where(core == 0, mine, got)
        high = jnp.where(core == 0, got, mine)
        return jnp.concatenate([low, high], axis=0)

    wo = pair_up(out_cols(core), swap(out_cols(1 - core)))
    wq = pair_up(qkv_cols(core), swap(qkv_cols(1 - core)))
    tok_other = swap(tokens)
    len_other = swap(page_lengths)

    wo_y = lax.dynamic_slice_in_dim(wo, grp * WY, WY, 1)
    wo_r = wo[:, SIDE * WY :]

    def line_a(v):
        return jnp.stack([v, move_a(v, 1), move_a(v, 2), move_a(v, -1)])

    def line_b(t):
        one = move_b(t, 1)
        three = move_b(t, -1)
        return (t, one, three, move_b(one[:2], 1), move_b(three[2:], -1))

    ty = line_a(wo_y)
    tq = line_a(wq)
    tr = line_a(wo_r)
    w4 = jnp.stack([ty, move_b(ty, 1), move_b(ty, 2), move_b(ty, -1)])
    y1 = move_y(w4, 1)
    y3 = move_y(w4, -1)
    y_pieces = (w4, y1, y3, move_y(y1[:2], 1), move_y(y3[2:], -1))
    q_pieces = line_b(tq)
    r_pieces = line_b(tr)

    labels = page_group[:, 0] * REPORTS + page_report
    all_labels = lax.all_gather(labels, ("grp", "page"), axis=0, tiled=True)

    gain = attn_gain[None, :]
    x_own = rms_scale(tokens, gain).astype(BF)
    x_other = rms_scale(tok_other, gain).astype(BF)
    seg_own = page_index(page_lengths[0], count)
    seg_other = page_index(len_other[0], count)
    seg_col = jnp.concatenate([seg_own, seg_other])[:, None]
    seg_row = jnp.stack([seg_own, seg_other])[:, None, :]
    att = page_qkv(order, x_own, x_other, seg_col, seg_row, q_pieces)
    att_in = swap(att)
    names = jnp.arange(pages, dtype=jnp.int32)[:, None]
    members = tuple((seg[None, :] == names).astype(BF) for seg in (seg_own, seg_other))
    lens = tuple(v[0][:, None].astype(F32) for v in (page_lengths, len_other))
    st_own, st_other, pool_own, pool_other = page_out(
        order, pos, tokens, tok_other, att, att_in, members, lens, y_pieces, r_pieces
    )

    def side_by_side(mine, got):
        left = jnp.where(core == 0, mine, got)
        right = jnp.where(core == 0, got, mine)
        return jnp.concatenate([left, right], axis=1)

    vectors = side_by_side(pool_own, swap(pool_other))
    token_states = side_by_side(st_own, swap(st_other))

    keys = rms_scale(vectors, doc_gain).astype(BF)
    heads = width // HD
    slots = 2 * SIDE * SIDE
    blocks = jnp.stack([vectors.reshape(pages, heads, HD), keys.reshape(pages, heads, HD)], axis=2)
    blocks = blocks.reshape(pages, heads, 2 * HD).transpose(1, 0, 2)
    blocks = jnp.pad(blocks, ((0, slots - heads), (0, 0), (0, 0)))
    blocks = jnp.broadcast_to(blocks[None], (SIDE,) + blocks.shape).reshape(-1, pages, 2 * HD)
    gathered = lax.all_to_all(blocks, ("grp", "page"), split_axis=0, concat_axis=0, tiled=True)
    plane = slots * pages
    label_col = lax.dynamic_slice_in_dim(all_labels, grp * plane, plane)[:, None]
    mixed = doc_attention(pos, gathered.reshape(-1, 2 * HD), label_col, all_labels[None, :])

    line = line_a(mixed)
    pieces = (line, move_b(line, 1), move_b(line, 2), move_b(line, -1))
    pieces_t = tuple(swap(v) for v in pieces)
    pick = (
        jnp.arange(plane, dtype=jnp.int32)[None, :] == page * pages + jnp.arange(pages)[:, None]
    ).astype(BF)
    own, other, states = feed_forward_call(
        order, order_t, dest, dest_t, pos, pieces, pieces_t, ffn_gain[None, :], gate_up_weight, w_down, pick
    )
    got = swap(other)

    def total(*terms):
        return sum(v.astype(F32) for v in terms)

    part = [total(own[j], got[j]).astype(BF) for j in range(SIDE)]
    part = total(part[0], *(move_a(part[j], j) for j in range(1, SIDE)))
    part = [part[k].astype(BF) if k else part[k] for k in range(SIDE)]
    summed = total(part[0], *(move_b(part[k], k) for k in range(1, SIDE)))
    page_embeddings = (states + summed).astype(BF)
    return (token_states, page_embeddings)


def feed_forward_call(order, order_t, dest, dest_t, pos, *rest):
    tables = jnp.concatenate([order, dest])
    tables_t = jnp.concatenate([order_t, dest_t])
    return feed_forward(tables, tables_t, pos, *rest)


def solution(mesh):
    in_specs = (
        P(("grp", "page"), None),
        P(("grp", "page"), None),
        P(("grp", "page"), None),
        P(("grp", "page")),
        P(),
        P("page", None),
        P("page", None),
        P("page", None),
        P(),
        P(),
        P(None, None, "page"),
        P("page", None),
    )
    out_specs = (P(("grp", "page"), None), P(("grp", "page"), None))
    return jax.shard_map(
        on_device, mesh=mesh, in_specs=in_specs, out_specs=out_specs, check_vma=False
    )
```

```python
import functools
import math

import jax
import jax.numpy as jnp
from jax import lax
from jax.experimental import pallas as pl
from jax.experimental.pallas import tpu as pltpu
from jax.sharding import PartitionSpec as P

HD = 128
REPORTS = 16
SIDE = 4
WY = 384
BF = jnp.bfloat16
F32 = jnp.float32
MIB = 1 << 20


def vmem():
    return pl.BlockSpec(memory_space=pltpu.VMEM)


def smem():
    return pl.BlockSpec(memory_space=pltpu.SMEM)


def anym():
    return pl.BlockSpec(memory_space=pl.ANY)


def params(mib):
    return pltpu.CompilerParams(vmem_limit_bytes=mib * MIB)


def chip_perm(step):
    pairs = []
    for x in range(SIDE):
        for z in range(SIDE):
            for c in range(2):
                a, b, d = step(x, z, c)
                pairs.append(((x * SIDE + z) * 2 + c, ((a % SIDE) * SIDE + b % SIDE) * 2 + d))
    return pairs


def swap(v):
    return lax.ppermute(v, "page", chip_perm(lambda x, z, c: (x, z, 1 - c)))


def move_a(v, k):
    return lax.ppermute(
        v, "page", chip_perm(lambda x, z, c: (x + k, z, c) if c == 0 else (x, z + k, c))
    )


def move_b(v, k):
    return lax.ppermute(
        v, "page", chip_perm(lambda x, z, c: (x, z + k, c) if c == 0 else (x + k, z, c))
    )


def rms_scale(values, gain):
    wide = values.astype(F32)
    return wide * lax.rsqrt(jnp.mean(wide * wide, axis=-1, keepdims=True) + 1e-06) * gain


def page_index(lengths, count):
    ends = jnp.cumsum(lengths, dtype=jnp.int32)
    position = jnp.arange(count, dtype=jnp.int32)
    return jnp.sum((position[:, None] >= ends[None, :]).astype(jnp.int32), axis=1)


def run_copies(copies, sems):
    started = []
    for i, (src, dst) in enumerate(copies):
        copy = pltpu.make_async_copy(src, dst, sems.at[i])
        copy.start()
        started.append(copy)
    return started


QKV_COLS = 1152
BLOCK = 256


def norm_kernel(tok, gain, out, wide_ref):
    chunk = 32
    depth = tok.shape[1] // out.shape[0]

    @pl.loop(0, tok.shape[0] // chunk)
    def _(i):
        rows = pl.ds(pl.multiple_of(i * chunk, chunk), chunk)
        wide = tok[rows, :].astype(F32)
        scale = lax.rsqrt(jnp.mean(wide * wide, axis=1, keepdims=True) + 1e-06)
        wide_ref[...] = wide * scale * gain[...]
        for n in range(out.shape[0]):
            piece = wide_ref[:, n * depth : (n + 1) * depth]
            pad = jnp.zeros((chunk, BLOCK - depth), F32)
            out[n, rows, :] = jnp.concatenate([piece, pad], axis=1).astype(BF)


def norm_blocks(tok, gain):
    count, width = tok.shape
    chips = SIDE * SIDE
    return pl.pallas_call(
        norm_kernel,
        out_shape=jax.ShapeDtypeStruct((chips, count, BLOCK), BF),
        in_specs=[vmem()] * 2,
        out_specs=vmem(),
        scratch_shapes=[pltpu.VMEM((32, width), F32)],
        compiler_params=params(24),
        cost_estimate=pl.CostEstimate(flops=0, bytes_accessed=4 * count * width, transcendentals=0),
    )(tok, gain)


def qkv_load(order, steps, pieces, xo, xt, w, x, sems):
    cols = w.shape[1]
    depth = pieces[0].shape[1]
    tokens = xo.shape[1]
    copies = []
    for n in range(2 * len(pieces)):
        piece = pieces[n // 2].at[n % 2, :, pl.ds(0, cols)]
        copies.append((piece, w.at[pl.ds(n * BLOCK, depth), :]))
    started = run_copies(copies, sems)
    for n in range(2 * len(pieces)):
        q = order[steps[n // SIDE] * SIDE + n % SIDE]
        x[0:tokens, n * BLOCK : (n + 1) * BLOCK] = xo[q]
        x[tokens : 2 * tokens, n * BLOCK : (n + 1) * BLOCK] = xt[q]
        w[n * BLOCK + depth : (n + 1) * BLOCK, :] = jnp.zeros((BLOCK - depth, cols), BF)
    for copy in started:
        copy.wait()


QKV_TILE = 384


def qkv_first_kernel(order, xo, xt, *refs):
    *pieces, part, w, x, sems = refs
    qkv_load(order, (0, 1, 3), pieces, xo, xt, w, x, sems)

    @pl.loop(0, part.shape[1] // QKV_TILE)
    def _(n):
        there = pl.ds(pl.multiple_of(n * QKV_TILE, 128), QKV_TILE)
        part[:, there] = jnp.dot(x[...], w[:, there], preferred_element_type=F32)


def qkv_last_kernel(order, xo, xt, seg_col, seg_row, part, *refs):
    *pieces, out, w, x, qkv, sems = refs
    qkv_load(order, (2,), pieces, xo, xt, w, x, sems)

    @pl.loop(0, part.shape[1] // QKV_TILE)
    def _(n):
        there = pl.ds(pl.multiple_of(n * QKV_TILE, 128), QKV_TILE)
        last = jnp.dot(x[...], w[:, there], preferred_element_type=F32)
        qkv[:, there] = (part[:, there] + last).astype(BF)

    heads = out.shape[1] // HD
    tokens = xo.shape[1]

    @pl.loop(0, 2)
    def _(b):
        rows = pl.ds(pl.multiple_of(b * tokens, tokens), tokens)
        same = seg_col[rows, :] == seg_row[b]
        keys = qkv[rows, heads * HD : (heads + 1) * HD]
        values = qkv[rows, (heads + 1) * HD : (heads + 2) * HD]
        for h in range(heads):
            query = qkv[rows, h * HD : (h + 1) * HD]
            scores = lax.dot_general(
                query, keys, (((1,), (1,)), ((), ())), preferred_element_type=F32
            ) * (math.log2(math.e) / math.sqrt(HD))
            scores = jnp.where(same, scores, -1e30)
            top = jnp.max(scores, axis=1, keepdims=True)
            e = jnp.exp2(scores - top)
            weights = (e * (1.0 / jnp.sum(e, axis=1, keepdims=True))).astype(BF)
            out[rows, h * HD : (h + 1) * HD] = jnp.dot(
                weights, values, preferred_element_type=F32
            ).astype(BF)


def qkv_first(order, x_own, x_other, pieces, cols):
    tokens = x_own.shape[1]
    return pl.pallas_call(
        qkv_first_kernel,
        out_shape=jax.ShapeDtypeStruct((2 * tokens, cols), F32),
        in_specs=[smem()] + [vmem()] * 2 + [anym()] * 6,
        out_specs=vmem(),
        scratch_shapes=[
            pltpu.VMEM((12 * BLOCK, cols), BF),
            pltpu.VMEM((2 * tokens, 12 * BLOCK), BF),
            pltpu.SemaphoreType.DMA((12,)),
        ],
        compiler_params=params(40),
        cost_estimate=pl.CostEstimate(
            flops=4 * tokens * 12 * BLOCK * cols, bytes_accessed=24 * BLOCK * cols, transcendentals=0
        ),
    )(order, x_own, x_other, *pieces)


def qkv_last(order, x_own, x_other, seg_col, seg_row, part, pieces):
    tokens = x_own.shape[1]
    cols = part.shape[1]
    return pl.pallas_call(
        qkv_last_kernel,
        out_shape=jax.ShapeDtypeStruct((2 * tokens, cols - 2 * HD), BF),
        in_specs=[smem()] + [vmem()] * 5 + [anym()] * 2,
        out_specs=vmem(),
        scratch_shapes=[
            pltpu.VMEM((4 * BLOCK, cols), BF),
            pltpu.VMEM((2 * tokens, 4 * BLOCK), BF),
            pltpu.VMEM((2 * tokens, cols), BF),
            pltpu.SemaphoreType.DMA((4,)),
        ],
        compiler_params=params(40),
        cost_estimate=pl.CostEstimate(
            flops=4 * tokens * 8 * BLOCK * cols, bytes_accessed=24 * BLOCK * cols, transcendentals=0
        ),
    )(order, x_own, x_other, seg_col, seg_row, part, *pieces)


def out_kernel(
    order, pos, tok_own, tok_other, att, att_in, member, member_t, inv, inv_t, w_all, *refs
):
    pieces, refs = refs[: 2 * SIDE], refs[2 * SIDE :]
    st_own, st_other, pool_own, pool_other, w, rest, full, sems = refs
    core = pos[0]
    depth, wy = w_all.shape[2:]
    tile = rest.shape[1] // 2
    chips = SIDE * SIDE
    copies = []
    rows = [pl.ds(pl.multiple_of(order[n] * depth, 16), depth) for n in range(chips)]
    for i in range(SIDE):
        for n in range(chips):
            copies.append((w_all.at[i, n], w.at[i, rows[n], :]))
    for n in range(chips):
        for t in range(2):
            copies.append(
                (
                    pieces[n // 2].at[n % 2, pl.ds(t * depth, depth), pl.ds(QKV_COLS, tile)],
                    rest.at[rows[n], pl.ds(t * tile, tile)],
                )
            )
    started = run_copies(copies, sems)
    tokens = tok_own.shape[0]
    half = att.shape[1]
    mine = pl.ds(pl.multiple_of(core * half, 128), half)
    theirs = pl.ds(pl.multiple_of((1 - core) * half, 128), half)
    full[:, mine] = att[...]
    full[0:tokens, theirs] = att_in[tokens : 2 * tokens, :]
    full[tokens : 2 * tokens, theirs] = att_in[0:tokens, :]
    width = st_own.shape[1]

    def columns(lo, n, weight):
        cols = slice(lo, lo + n)
        there = pl.ds(pl.multiple_of(core * width + lo, 128), n)
        projected = jnp.dot(full[...], weight, preferred_element_type=F32)
        for first, tok, st, mem, ratio, pool in (
            (0, tok_own, st_own, member, inv, pool_own),
            (tokens, tok_other, st_other, member_t, inv_t, pool_other),
        ):
            states = (tok[:, there].astype(F32) + projected[first : first + tokens]).astype(BF)
            st[:, cols] = states
            pool[:, cols] = (
                jnp.dot(mem[...], states, preferred_element_type=F32) / ratio[...]
            ).astype(BF)

    for i in range(SIDE):
        for copy in started[i * chips : (i + 1) * chips]:
            copy.wait()
        columns(i * wy, wy, w[i])
    for copy in started[SIDE * chips :]:
        copy.wait()
    columns(SIDE * wy, 2 * tile, rest[...])


def page_out(order, pos, tok_own, tok_other, att, att_in, members, lens, w_all, pieces):
    tokens, width = tok_own.shape
    width = width // 2
    depth, wy = w_all.shape[2:]
    rows = SIDE * SIDE * depth
    pages = members[0].shape[0]
    st = jax.ShapeDtypeStruct((tokens, width), BF)
    pool = jax.ShapeDtypeStruct((pages, width), BF)
    return pl.pallas_call(
        out_kernel,
        out_shape=(st, st, pool, pool),
        in_specs=[smem()] * 2 + [vmem()] * 8 + [anym()] * 9,
        out_specs=(vmem(),) * 4,
        scratch_shapes=[
            pltpu.VMEM((SIDE, rows, wy), BF),
            pltpu.VMEM((rows, width - SIDE * wy), BF),
            pltpu.VMEM((2 * tokens, rows), BF),
            pltpu.SemaphoreType.DMA((6 * SIDE * SIDE,)),
        ],
        compiler_params=params(40),
        cost_estimate=pl.CostEstimate(
            flops=2 * 2 * tokens * width * rows, bytes_accessed=2 * width * rows, transcendentals=0
        ),
    )(order, pos, tok_own, tok_other, att, att_in, *members, *lens, w_all, *pieces)


def block_kernel(vec, label, out):
    pages, width = vec.shape
    wide = vec[...].astype(F32)
    scale = lax.rsqrt(jnp.mean(wide * wide, axis=1, keepdims=True) + 1e-06)
    high = scale.astype(BF)
    low = (scale - high.astype(F32)).astype(BF)
    lane = lax.broadcasted_iota(jnp.int32, (pages, HD), 1)
    side = jnp.where(lane == 0, high.astype(F32), jnp.where(lane == 1, low.astype(F32), 0.0))
    side = jnp.where(lane == 2, label[...].astype(F32), side).astype(BF)
    for h in range(width // HD):
        out[h, :, 0:HD] = vec[:, h * HD : (h + 1) * HD]
        out[h, :, HD : 2 * HD] = side
    for h in range(width // HD, out.shape[0]):
        out[h] = jnp.zeros((pages, 2 * HD), BF)


def page_blocks(vectors, labels, slots):
    return pl.pallas_call(
        block_kernel,
        out_shape=jax.ShapeDtypeStruct((slots, vectors.shape[0], 2 * HD), BF),
        in_specs=[vmem()] * 2,
        out_specs=vmem(),
        compiler_params=params(16),
    )(vectors, labels)


def doc_kernel(pos, rows, gain, out, keys_ref):
    count = out.shape[0]
    every = rows.shape[0]
    start = pl.multiple_of(pos[1] * count, count)
    mine = pl.ds(start, count)
    side = rows[:, HD : 2 * HD].astype(F32)
    scale = side[:, 0:1] + side[:, 1:2]
    keys = (rows[:, 0:HD].astype(F32) * scale * gain[...]).astype(BF)
    keys_ref[...] = keys
    query = keys_ref[mine, :]
    pick = (lax.broadcasted_iota(jnp.int32, (8, HD), 1) == 2).astype(BF)
    label_row = lax.dot_general(
        pick, rows[:, HD : 2 * HD], (((1,), (1,)), ((), ())), preferred_element_type=F32
    )[0:1, :]
    label_col = rows[mine, HD : 2 * HD].astype(F32)[:, 2:3]
    scores = lax.dot_general(
        query, keys, (((1,), (1,)), ((), ())), preferred_element_type=F32
    ) * (math.log2(math.e) / HD)
    scores = jnp.where(label_col == label_row, scores, -1e30)
    top = jnp.max(scores, axis=1, keepdims=True)
    e = jnp.exp2(scores - top)
    weights = (e * (1.0 / jnp.sum(e, axis=1, keepdims=True))).astype(BF)
    context = jnp.dot(weights, keys, preferred_element_type=F32)
    out[...] = (rows[mine, 0:HD].astype(F32) + context).astype(BF)


def doc_attention(pos, rows, gain, count):
    return pl.pallas_call(
        doc_kernel,
        out_shape=jax.ShapeDtypeStruct((count, HD), BF),
        in_specs=[smem()] + [vmem()] * 2,
        out_specs=vmem(),
        scratch_shapes=[pltpu.VMEM((rows.shape[0], HD), BF)],
        compiler_params=params(24),
    )(pos, rows, gain)


def ffn_kernel(
    order, order_t, pos, t, b1, b2, b3, tt, c1, c2, c3, gain, gate_up, down, pick,
    own, other, states, x, mixed, hidden, wgu, wd, acc, sems,
):
    core = pos[0]
    width = gain.shape[1]
    units = hidden.shape[1]
    half = units // 2
    weights = []
    n_sem = 32
    for n in range(2):
        for g in range(2):
            weights.append(
                pltpu.make_async_copy(
                    gate_up.at[g, :, n * half : (n + 1) * half],
                    wgu.at[g, :, n * half : (n + 1) * half],
                    sems.at[n_sem + 2 * n + g],
                )
            )
    down_copy = pltpu.make_async_copy(down, wd, sems.at[n_sem + 4])
    copies = []
    for table, side, pieces in ((order, core, (t, b1, b2, b3)), (order_t, 1 - core, (tt, c1, c2, c3))):
        for k, piece in enumerate(pieces):
            for j in range(SIDE):
                head = table[k * SIDE + j] * 2 + side
                copies.append((piece.at[j], x.at[:, pl.ds(pl.multiple_of(head * HD, HD), HD)]))
    started = run_copies(copies, sems)
    for copy in weights:
        copy.start()
    down_copy.start()
    for copy in started:
        copy.wait()
    chunk = 32

    @pl.loop(0, x.shape[0] // chunk)
    def _(i):
        rows = pl.ds(pl.multiple_of(i * chunk, chunk), chunk)
        wide = x[rows, 0:width].astype(F32)
        scale = lax.rsqrt(jnp.mean(wide * wide, axis=1, keepdims=True) + 1e-06)
        mixed[rows, :] = (wide * scale * gain[...]).astype(BF)

    for n in range(2):
        weights[2 * n].wait()
        weights[2 * n + 1].wait()
        cols = slice(n * half, (n + 1) * half)
        gate = jnp.dot(mixed[...], wgu[0, :, cols], preferred_element_type=F32)
        up = jnp.dot(mixed[...], wgu[1, :, cols], preferred_element_type=F32)
        hidden[:, cols] = (gate * jax.nn.sigmoid(gate) * up).astype(BF)
    down_copy.wait()
    tile = 512
    pages = acc.shape[1]

    @pl.loop(0, width // tile)
    def _(n):
        cols = pl.ds(pl.multiple_of(n * tile, 128), tile)
        part = jnp.dot(hidden[...], wd[:, cols], preferred_element_type=F32)
        acc[...] = part.reshape(acc.shape)
        for k in range(SIDE):
            for j in range(SIDE):
                own[j, k, :, cols] = acc[order[16 + k * SIDE + j] * 2 + core].astype(BF)
                other[j, k, :, cols] = acc[order_t[16 + k * SIDE + j] * 2 + 1 - core].astype(BF)
        states[:, cols] = jnp.dot(pick[...], x[:, cols], preferred_element_type=F32)


def feed_forward(order, order_t, pos, pieces, pieces_t, gain, gate_up, down, pick):
    width = gain.shape[1]
    units = down.shape[0]
    pages, count = pick.shape
    part = jax.ShapeDtypeStruct((SIDE, SIDE, pages, width), BF)
    return pl.pallas_call(
        ffn_kernel,
        out_shape=(part, part, jax.ShapeDtypeStruct((pages, width), F32)),
        in_specs=[smem()] * 3 + [anym()] * 8 + [vmem()] + [anym()] * 2 + [vmem()],
        out_specs=(vmem(),) * 3,
        scratch_shapes=[
            pltpu.VMEM((count, 2 * SIDE * SIDE * HD), BF),
            pltpu.VMEM((count, width), BF),
            pltpu.VMEM((count, units), BF),
            pltpu.VMEM((2, width, units), BF),
            pltpu.VMEM((units, width), BF),
            pltpu.VMEM((count // pages, pages, 512), F32),
            pltpu.SemaphoreType.DMA((40,)),
        ],
        compiler_params=params(40),
        cost_estimate=pl.CostEstimate(
            flops=6 * count * width * units, bytes_accessed=6 * width * units, transcendentals=0
        ),
    )(order, order_t, pos, *pieces, *pieces_t, gain, gate_up, down, pick)


def on_device(
    tokens,
    page_lengths,
    page_group,
    page_report,
    attn_gain,
    w_query,
    w_keyval,
    w_out,
    doc_gain,
    ffn_gain,
    gate_up_weight,
    w_down,
):
    count, width = tokens.shape
    pages = page_lengths.shape[1]
    grp = lax.axis_index("grp")
    page = lax.axis_index("page")
    core = page % 2
    z = (page // 2) % SIDE
    x = page // (2 * SIDE)
    pos = jnp.stack([core, grp]).astype(jnp.int32)
    step = jnp.arange(SIDE, dtype=jnp.int32)
    zero_order = (((x - step) % SIDE)[None, :] * SIDE + ((z - step) % SIDE)[:, None]).reshape(-1)
    one_order = (((x - step) % SIDE)[:, None] * SIDE + ((z - step) % SIDE)[None, :]).reshape(-1)
    order = jnp.where(core == 0, zero_order, one_order)
    order_t = jnp.where(core == 0, one_order, zero_order)
    zero_dest = (((x + step) % SIDE)[None, :] * SIDE + ((z + step) % SIDE)[:, None]).reshape(-1)
    one_dest = (((x + step) % SIDE)[:, None] * SIDE + ((z + step) % SIDE)[None, :]).reshape(-1)
    dest = jnp.where(core == 0, zero_dest, one_dest)
    dest_t = jnp.where(core == 0, one_dest, zero_dest)

    out_half = w_out.shape[1] // 2
    q_half = w_query.shape[1] // 2

    def out_cols(c):
        return lax.dynamic_slice_in_dim(w_out, c * out_half, out_half, 1)

    def qkv_cols(c):
        return jnp.concatenate(
            [
                lax.dynamic_slice_in_dim(w_query, c * q_half, q_half, 1),
                lax.dynamic_slice_in_dim(w_keyval, c * HD, HD, 1),
                lax.dynamic_slice_in_dim(w_keyval, (2 + c) * HD, HD, 1),
            ],
            axis=1,
        )

    def pair_up(mine, got):
        low = jnp.where(core == 0, mine, got)
        high = jnp.where(core == 0, got, mine)
        return jnp.concatenate([low, high], axis=0)

    wo = pair_up(out_cols(core), swap(out_cols(1 - core)))
    wq = pair_up(qkv_cols(core), swap(qkv_cols(1 - core)))
    wo_y = lax.dynamic_slice_in_dim(wo, grp * WY, WY, 1)
    tile = (out_half - SIDE * WY) // 2
    wo_r = wo[:, SIDE * WY :]
    wq = jnp.concatenate([wq, jnp.concatenate([wo_r[:, :tile], wo_r[:, tile:]], axis=0)], axis=1)

    tok_other = swap(tokens)
    len_other = swap(page_lengths)
    gain = attn_gain[None, :]
    x_own = norm_blocks(tokens, gain)
    x_other = norm_blocks(tok_other, gain)
    seg_own = page_index(page_lengths[0], count)
    seg_other = page_index(len_other[0], count)
    seg_col = jnp.concatenate([seg_own, seg_other])[:, None]
    seg_row = jnp.stack([seg_own, seg_other])[:, None, :]
    names = jnp.arange(pages, dtype=jnp.int32)[:, None]
    members = tuple((seg[None, :] == names).astype(BF) for seg in (seg_own, seg_other))
    lens = tuple(v[0][:, None].astype(F32) for v in (page_lengths, len_other))
    slots = 2 * SIDE * SIDE
    plane = slots * pages
    labels = page_group * REPORTS + page_report[:, None]
    head_gain = jnp.pad(doc_gain, (0, slots * HD - width))
    head_gain = lax.dynamic_slice_in_dim(head_gain, page * HD, HD)[None, :]
    pick = (
        jnp.arange(plane, dtype=jnp.int32)[None, :] == page * pages + jnp.arange(pages)[:, None]
    ).astype(BF)
    tables = jnp.concatenate([order, dest])
    tables_t = jnp.concatenate([order_t, dest_t])
    early = (
        x_own, x_other, seg_col, seg_row, members, lens, labels, head_gain, pick,
        tables, tables_t, pos, ffn_gain[None, :],
    )

    line_y = jnp.stack([wo_y, move_a(wo_y, 1), move_a(wo_y, 2), move_a(wo_y, -1)])
    line_y, wq = lax.optimization_barrier((line_y, wq))
    square = (line_y, move_b(line_y, 1), move_b(line_y, 2), move_b(line_y, -1))
    q1, q3 = move_a(wq, 1), move_a(wq, -1)
    square, q1, q3 = lax.optimization_barrier((square, q1, q3))
    wo_all = lax.all_gather(jnp.concatenate(square), "grp", axis=0, tiled=True)
    wo_all = wo_all.reshape((SIDE, SIDE * SIDE) + wo_y.shape)
    low = jnp.stack([wq, q1])
    high = jnp.stack([move_a(wq, 2), q3])
    up = [move_b(low, 1), move_b(high, 1)]
    down = [move_b(low, -1), move_b(high, -1)]
    up[0], early = lax.optimization_barrier((up[0], early))
    far = [move_b(up[0], 1), move_b(down[1], -1)]
    pieces = [low, high] + up + far + down
    (
        x_own, x_other, seg_col, seg_row, members, lens, labels, head_gain, pick,
        tables, tables_t, pos, ffn_row,
    ) = early

    part = qkv_first(tables, x_own, x_other, pieces[:4] + pieces[6:], QKV_COLS)
    att = qkv_last(tables, x_own, x_other, seg_col, seg_row, part, far)
    att_in = swap(att)
    st_own, st_other, pool_own, pool_other = page_out(
        tables, pos, tokens, tok_other, att, att_in, members, lens, wo_all, pieces
    )

    def side_by_side(mine, got):
        left = jnp.where(core == 0, mine, got)
        right = jnp.where(core == 0, got, mine)
        return jnp.concatenate([left, right], axis=1)

    vectors = side_by_side(pool_own, swap(pool_other))
    token_states = side_by_side(st_own, swap(st_other))

    blocks = page_blocks(vectors, labels, slots)
    blocks = jnp.broadcast_to(blocks[None], (SIDE,) + blocks.shape).reshape(-1, pages, 2 * HD)
    gathered = lax.all_to_all(blocks, ("grp", "page"), split_axis=0, concat_axis=0, tiled=True)
    mixed = doc_attention(pos, gathered.reshape(-1, 2 * HD), head_gain, plane)

    line = jnp.stack([mixed, move_a(mixed, 1), move_a(mixed, 2), move_a(mixed, -1)])
    pieces = (line, move_b(line, 1), move_b(line, 2), move_b(line, -1))
    pieces_t = tuple(swap(v) for v in pieces)
    own, other, states = feed_forward(
        tables, tables_t, pos, pieces, pieces_t, ffn_row, gate_up_weight, w_down, pick
    )
    got = swap(other)

    def total(*terms):
        return sum(v.astype(F32) for v in terms)

    part = [total(own[j], got[j]).astype(BF) for j in range(SIDE)]
    part = total(part[0], *(move_a(part[j], j) for j in range(1, SIDE)))
    part = [part[k].astype(BF) if k else part[k] for k in range(SIDE)]
    summed = total(part[0], *(move_b(part[k], k) for k in range(1, SIDE)))
    page_embeddings = (states + summed).astype(BF)
    return (token_states, page_embeddings)


def solution(mesh):
    in_specs = (
        P(("grp", "page"), None),
        P(("grp", "page"), None),
        P(("grp", "page"), None),
        P(("grp", "page")),
        P(),
        P("page", None),
        P("page", None),
        P("page", None),
        P(),
        P(),
        P(None, None, "page"),
        P("page", None),
    )
    out_specs = (P(("grp", "page"), None), P(("grp", "page"), None))
    return jax.shard_map(
        on_device, mesh=mesh, in_specs=in_specs, out_specs=out_specs, check_vma=False
    )
```

```python
import functools
import math

import jax
import jax.numpy as jnp
from jax import lax
from jax.experimental import pallas as pl
from jax.experimental.pallas import tpu as pltpu
from jax.sharding import PartitionSpec as P

HD = 128
REPORTS = 16
SIDE = 4
WY = 384
BF = jnp.bfloat16
F32 = jnp.float32
MIB = 1 << 20


def vmem():
    return pl.BlockSpec(memory_space=pltpu.VMEM)


def smem():
    return pl.BlockSpec(memory_space=pltpu.SMEM)


def anym():
    return pl.BlockSpec(memory_space=pl.ANY)


def params(mib):
    return pltpu.CompilerParams(vmem_limit_bytes=mib * MIB)


def chip_perm(step):
    pairs = []
    for x in range(SIDE):
        for z in range(SIDE):
            for c in range(2):
                a, b, d = step(x, z, c)
                pairs.append(((x * SIDE + z) * 2 + c, ((a % SIDE) * SIDE + b % SIDE) * 2 + d))
    return pairs


def swap(v):
    return lax.ppermute(v, "page", chip_perm(lambda x, z, c: (x, z, 1 - c)))


def move_a(v, k):
    return lax.ppermute(
        v, "page", chip_perm(lambda x, z, c: (x + k, z, c) if c == 0 else (x, z + k, c))
    )


def move_b(v, k):
    return lax.ppermute(
        v, "page", chip_perm(lambda x, z, c: (x, z + k, c) if c == 0 else (x + k, z, c))
    )


def rms_scale(values, gain):
    wide = values.astype(F32)
    return wide * lax.rsqrt(jnp.mean(wide * wide, axis=-1, keepdims=True) + 1e-06) * gain


def page_index(lengths, count):
    ends = jnp.cumsum(lengths, dtype=jnp.int32)
    position = jnp.arange(count, dtype=jnp.int32)
    return jnp.sum((position[:, None] >= ends[None, :]).astype(jnp.int32), axis=1)


def chip_at(pos, core, j, k, sign):
    shift_x = jnp.where(core == 0, sign * j, sign * k)
    shift_z = jnp.where(core == 0, sign * k, sign * j)
    return lax.rem(pos[2] + SIDE + shift_x, SIDE) * SIDE + lax.rem(pos[3] + SIDE + shift_z, SIDE)


def run_copies(copies, sems):
    started = []
    for i, (src, dst) in enumerate(copies):
        copy = pltpu.make_async_copy(src, dst, sems.at[i])
        copy.start()
        started.append(copy)
    return started


QKV_COLS = 1152
BLOCK = 256


def norm_kernel(tok, gain, out, wide_ref):
    chunk = 32
    depth = tok.shape[1] // out.shape[0]

    @pl.loop(0, tok.shape[0] // chunk)
    def _(i):
        rows = pl.ds(pl.multiple_of(i * chunk, chunk), chunk)
        wide = tok[rows, :].astype(F32)
        scale = lax.rsqrt(jnp.mean(wide * wide, axis=1, keepdims=True) + 1e-06)
        wide_ref[...] = wide * scale * gain[...]
        for n in range(out.shape[0]):
            piece = wide_ref[:, n * depth : (n + 1) * depth]
            pad = jnp.zeros((chunk, BLOCK - depth), F32)
            out[n, rows, :] = jnp.concatenate([piece, pad], axis=1).astype(BF)


def norm_blocks(tok, gain):
    count, width = tok.shape
    chips = SIDE * SIDE
    return pl.pallas_call(
        norm_kernel,
        out_shape=jax.ShapeDtypeStruct((chips, count, BLOCK), BF),
        in_specs=[vmem()] * 2,
        out_specs=vmem(),
        scratch_shapes=[pltpu.VMEM((32, width), F32)],
        compiler_params=params(24),
        cost_estimate=pl.CostEstimate(flops=0, bytes_accessed=4 * count * width, transcendentals=0),
    )(tok, gain)


def qkv_load(pos, steps, pieces, xo, xt, w, x, sems):
    cols = w.shape[1]
    depth = pieces[0].shape[1]
    tokens = xo.shape[1]
    copies = []
    for n in range(2 * len(pieces)):
        piece = pieces[n // 2].at[n % 2, :, pl.ds(0, cols)]
        copies.append((piece, w.at[pl.ds(n * BLOCK, depth), :]))
    started = run_copies(copies, sems)
    for n in range(2 * len(pieces)):
        q = chip_at(pos, pos[0], n % SIDE, steps[n // SIDE], -1)
        x[0:tokens, n * BLOCK : (n + 1) * BLOCK] = xo[q]
        x[tokens : 2 * tokens, n * BLOCK : (n + 1) * BLOCK] = xt[q]
        w[n * BLOCK + depth : (n + 1) * BLOCK, :] = jnp.zeros((BLOCK - depth, cols), BF)
    for copy in started:
        copy.wait()


QKV_TILE = 384


def qkv_first_kernel(pos, xo, xt, *refs):
    *pieces, part, w, x, sems = refs
    qkv_load(pos, (0, 1, 3), pieces, xo, xt, w, x, sems)

    @pl.loop(0, part.shape[1] // QKV_TILE)
    def _(n):
        there = pl.ds(pl.multiple_of(n * QKV_TILE, 128), QKV_TILE)
        part[:, there] = jnp.dot(x[...], w[:, there], preferred_element_type=F32)


def qkv_last_kernel(pos, xo, xt, seg_col, seg_row, part, *refs):
    *pieces, out, w, x, qkv, sems = refs
    qkv_load(pos, (2,), pieces, xo, xt, w, x, sems)

    @pl.loop(0, part.shape[1] // QKV_TILE)
    def _(n):
        there = pl.ds(pl.multiple_of(n * QKV_TILE, 128), QKV_TILE)
        last = jnp.dot(x[...], w[:, there], preferred_element_type=F32)
        qkv[:, there] = (part[:, there] + last).astype(BF)

    heads = out.shape[1] // HD
    tokens = xo.shape[1]

    @pl.loop(0, 2)
    def _(b):
        rows = pl.ds(pl.multiple_of(b * tokens, tokens), tokens)
        same = seg_col[rows, :] == seg_row[b]
        keys = qkv[rows, heads * HD : (heads + 1) * HD]
        values = jnp.concatenate(
            [qkv[rows, (heads + 1) * HD : (heads + 2) * HD], jnp.ones((tokens, HD), BF)], axis=1
        )
        for h in range(heads):
            query = qkv[rows, h * HD : (h + 1) * HD]
            scores = lax.dot_general(
                query, keys, (((1,), (1,)), ((), ())), preferred_element_type=F32
            ) * (math.log2(math.e) / math.sqrt(HD))
            scores = jnp.where(same, scores, -1e30)
            top = jnp.max(scores, axis=1, keepdims=True)
            weights = jnp.exp2(scores - top).astype(BF)
            mixed = jnp.dot(weights, values, preferred_element_type=F32)
            out[rows, h * HD : (h + 1) * HD] = (mixed[:, 0:HD] / mixed[:, HD : 2 * HD]).astype(BF)


def qkv_first(pos, x_own, x_other, pieces, cols):
    tokens = x_own.shape[1]
    return pl.pallas_call(
        qkv_first_kernel,
        out_shape=jax.ShapeDtypeStruct((2 * tokens, cols), F32),
        in_specs=[smem()] + [vmem()] * 2 + [anym()] * 6,
        out_specs=vmem(),
        scratch_shapes=[
            pltpu.VMEM((12 * BLOCK, cols), BF),
            pltpu.VMEM((2 * tokens, 12 * BLOCK), BF),
            pltpu.SemaphoreType.DMA((12,)),
        ],
        compiler_params=params(40),
        cost_estimate=pl.CostEstimate(
            flops=4 * tokens * 12 * BLOCK * cols, bytes_accessed=24 * BLOCK * cols, transcendentals=0
        ),
    )(pos, x_own, x_other, *pieces)


def qkv_last(pos, x_own, x_other, seg_col, seg_row, part, pieces):
    tokens = x_own.shape[1]
    cols = part.shape[1]
    return pl.pallas_call(
        qkv_last_kernel,
        out_shape=jax.ShapeDtypeStruct((2 * tokens, cols - 2 * HD), BF),
        in_specs=[smem()] + [vmem()] * 5 + [anym()] * 2,
        out_specs=vmem(),
        scratch_shapes=[
            pltpu.VMEM((4 * BLOCK, cols), BF),
            pltpu.VMEM((2 * tokens, 4 * BLOCK), BF),
            pltpu.VMEM((2 * tokens, cols), BF),
            pltpu.SemaphoreType.DMA((4,)),
        ],
        compiler_params=params(40),
        cost_estimate=pl.CostEstimate(
            flops=4 * tokens * 8 * BLOCK * cols, bytes_accessed=24 * BLOCK * cols, transcendentals=0
        ),
    )(pos, x_own, x_other, seg_col, seg_row, part, *pieces)


def arrange_kernel(pos, t, b1, b2, b3, out):
    for k, piece in enumerate((t, b1, b2, b3)):
        for j in range(SIDE):
            out[chip_at(pos, pos[0], j, k, -1)] = piece[j]


def arrange(pos, pieces):
    n, rows, cols = pieces[0].shape
    return pl.pallas_call(
        arrange_kernel,
        out_shape=jax.ShapeDtypeStruct((SIDE * n, rows, cols), BF),
        in_specs=[smem()] + [vmem()] * 4,
        out_specs=vmem(),
        compiler_params=params(16),
        cost_estimate=pl.CostEstimate(
            flops=0, bytes_accessed=4 * SIDE * n * rows * cols, transcendentals=0
        ),
    )(pos, *pieces)


def out_kernel(
    pos, tok_own, tok_other, att, att_in, member, member_t, inv, inv_t, w_all, *refs
):
    pieces, refs = refs[: 2 * SIDE], refs[2 * SIDE :]
    st_own, st_other, pool_own, pool_other, w, rest, full, sems = refs
    core = pos[0]
    wy = w_all.shape[2]
    depth = pieces[0].shape[1] // 2
    tile = rest.shape[1] // 2
    chips = SIDE * SIDE
    copies = []
    rows = [
        pl.ds(pl.multiple_of(chip_at(pos, core, n % SIDE, n // SIDE, -1) * depth, 16), depth)
        for n in range(chips)
    ]
    for i in range(SIDE):
        copies.append((w_all.at[i], w.at[i]))
    for n in range(chips):
        for t in range(2):
            copies.append(
                (
                    pieces[n // 2].at[n % 2, pl.ds(t * depth, depth), pl.ds(QKV_COLS, tile)],
                    rest.at[rows[n], pl.ds(t * tile, tile)],
                )
            )
    started = run_copies(copies, sems)
    tokens = tok_own.shape[0]
    half = att.shape[1]
    mine = pl.ds(pl.multiple_of(core * half, 128), half)
    theirs = pl.ds(pl.multiple_of((1 - core) * half, 128), half)
    full[:, mine] = att[...]
    full[0:tokens, theirs] = att_in[tokens : 2 * tokens, :]
    full[tokens : 2 * tokens, theirs] = att_in[0:tokens, :]
    width = st_own.shape[1]

    def columns(lo, n, weight):
        cols = slice(lo, lo + n)
        there = pl.ds(pl.multiple_of(core * width + lo, 128), n)
        projected = jnp.dot(full[...], weight, preferred_element_type=F32)
        for first, tok, st, mem, ratio, pool in (
            (0, tok_own, st_own, member, inv, pool_own),
            (tokens, tok_other, st_other, member_t, inv_t, pool_other),
        ):
            states = (tok[:, there].astype(F32) + projected[first : first + tokens]).astype(BF)
            st[:, cols] = states
            pool[:, cols] = (
                jnp.dot(mem[...], states, preferred_element_type=F32) / ratio[...]
            ).astype(BF)

    for i in range(SIDE):
        started[i].wait()
        columns(i * wy, wy, w[i])
    for copy in started[SIDE:]:
        copy.wait()
    columns(SIDE * wy, 2 * tile, rest[...])


def page_out(pos, tok_own, tok_other, att, att_in, members, lens, w_all, pieces):
    tokens, width = tok_own.shape
    width = width // 2
    rows, wy = w_all.shape[1:]
    pages = members[0].shape[0]
    st = jax.ShapeDtypeStruct((tokens, width), BF)
    pool = jax.ShapeDtypeStruct((pages, width), BF)
    return pl.pallas_call(
        out_kernel,
        out_shape=(st, st, pool, pool),
        in_specs=[smem()] + [vmem()] * 8 + [anym()] * 9,
        out_specs=(vmem(),) * 4,
        scratch_shapes=[
            pltpu.VMEM((SIDE, rows, wy), BF),
            pltpu.VMEM((rows, width - SIDE * wy), BF),
            pltpu.VMEM((2 * tokens, rows), BF),
            pltpu.SemaphoreType.DMA((SIDE + 2 * SIDE * SIDE,)),
        ],
        compiler_params=params(40),
        cost_estimate=pl.CostEstimate(
            flops=2 * 2 * tokens * width * rows, bytes_accessed=2 * width * rows, transcendentals=0
        ),
    )(pos, tok_own, tok_other, att, att_in, *members, *lens, w_all, *pieces)


def block_kernel(vec, label, out):
    pages, width = vec.shape
    wide = vec[...].astype(F32)
    scale = lax.rsqrt(jnp.mean(wide * wide, axis=1, keepdims=True) + 1e-06)
    high = scale.astype(BF)
    low = (scale - high.astype(F32)).astype(BF)
    lane = lax.broadcasted_iota(jnp.int32, (pages, HD), 1)
    side = jnp.where(lane == 0, high.astype(F32), jnp.where(lane == 1, low.astype(F32), 0.0))
    side = jnp.where(lane == 2, label[...].astype(F32), side).astype(BF)
    for h in range(width // HD):
        out[h, :, 0:HD] = vec[:, h * HD : (h + 1) * HD]
        out[h, :, HD : 2 * HD] = side
    for h in range(width // HD, out.shape[0]):
        out[h] = jnp.zeros((pages, 2 * HD), BF)


def page_blocks(vectors, labels, slots):
    return pl.pallas_call(
        block_kernel,
        out_shape=jax.ShapeDtypeStruct((slots, vectors.shape[0], 2 * HD), BF),
        in_specs=[vmem()] * 2,
        out_specs=vmem(),
        compiler_params=params(16),
    )(vectors, labels)


def doc_kernel(pos, rows, gain, out, keys_ref):
    count = out.shape[0]
    every = rows.shape[0]
    start = pl.multiple_of(pos[1] * count, count)
    mine = pl.ds(start, count)
    side = rows[:, HD : 2 * HD].astype(F32)
    scale = side[:, 0:1] + side[:, 1:2]
    keys = (rows[:, 0:HD].astype(F32) * scale * gain[...]).astype(BF)
    keys_ref[...] = keys
    query = keys_ref[mine, :]
    pick = (lax.broadcasted_iota(jnp.int32, (8, HD), 1) == 2).astype(BF)
    label_row = lax.dot_general(
        pick, rows[:, HD : 2 * HD], (((1,), (1,)), ((), ())), preferred_element_type=F32
    )[0:1, :]
    label_col = rows[mine, HD : 2 * HD].astype(F32)[:, 2:3]
    scores = lax.dot_general(
        query, keys, (((1,), (1,)), ((), ())), preferred_element_type=F32
    ) * (math.log2(math.e) / HD)
    scores = jnp.where(label_col == label_row, scores, -1e30)
    top = jnp.max(scores, axis=1, keepdims=True)
    e = jnp.exp2(scores - top)
    weights = (e * (1.0 / jnp.sum(e, axis=1, keepdims=True))).astype(BF)
    context = jnp.dot(weights, keys, preferred_element_type=F32)
    out[...] = (rows[mine, 0:HD].astype(F32) + context).astype(BF)


def doc_attention(pos, rows, gain, count):
    return pl.pallas_call(
        doc_kernel,
        out_shape=jax.ShapeDtypeStruct((count, HD), BF),
        in_specs=[smem()] + [vmem()] * 2,
        out_specs=vmem(),
        scratch_shapes=[pltpu.VMEM((rows.shape[0], HD), BF)],
        compiler_params=params(24),
    )(pos, rows, gain)


def ffn_kernel(
    pos, t, b1, b2, b3, tt, c1, c2, c3, gain, gate_up, down, pick,
    own, other, states, x, mixed, hidden, wgu, wd, acc, sems,
):
    core = pos[0]
    width = gain.shape[1]
    units = hidden.shape[1]
    half = units // 2
    weights = []
    for n in range(2):
        for g in range(2):
            part = (g, slice(None), slice(n * half, (n + 1) * half))
            weights.append((gate_up.at[part], wgu.at[part]))
    weights.append((down, wd))
    copies = []
    for side, pieces in ((core, (t, b1, b2, b3)), (1 - core, (tt, c1, c2, c3))):
        for k, piece in enumerate(pieces):
            for j in range(SIDE):
                head = chip_at(pos, side, j, k, -1) * 2 + side
                copies.append((piece.at[j], x.at[:, pl.ds(pl.multiple_of(head * HD, HD), HD)]))
    started = run_copies(copies + weights, sems)
    weights = started[len(copies) :]
    for copy in started[: len(copies)]:
        copy.wait()
    chunk = 32

    @pl.loop(0, x.shape[0] // chunk)
    def _(i):
        rows = pl.ds(pl.multiple_of(i * chunk, chunk), chunk)
        wide = x[rows, 0:width].astype(F32)
        scale = lax.rsqrt(jnp.mean(wide * wide, axis=1, keepdims=True) + 1e-06)
        mixed[rows, :] = (wide * scale * gain[...]).astype(BF)

    for n in range(2):
        weights[2 * n].wait()
        weights[2 * n + 1].wait()
        cols = slice(n * half, (n + 1) * half)
        gate = jnp.dot(mixed[...], wgu[0, :, cols], preferred_element_type=F32)
        up = jnp.dot(mixed[...], wgu[1, :, cols], preferred_element_type=F32)
        hidden[:, cols] = (gate * jax.nn.sigmoid(gate) * up).astype(BF)
    weights[4].wait()
    tile = 512

    @pl.loop(0, width // tile)
    def _(n):
        cols = pl.ds(pl.multiple_of(n * tile, 128), tile)
        part = jnp.dot(hidden[...], wd[:, cols], preferred_element_type=F32)
        acc[...] = part.reshape(acc.shape)
        for k in range(SIDE):
            for j in range(SIDE):
                own[j, k, :, cols] = acc[chip_at(pos, core, j, k, 1) * 2 + core].astype(BF)
                other[j, k, :, cols] = acc[chip_at(pos, 1 - core, j, k, 1) * 2 + 1 - core].astype(BF)
        states[:, cols] = jnp.dot(pick[...], x[:, cols], preferred_element_type=F32)


def feed_forward(pos, pieces, pieces_t, gain, gate_up, down, pick):
    width = gain.shape[1]
    units = down.shape[0]
    pages, count = pick.shape
    part = jax.ShapeDtypeStruct((SIDE, SIDE, pages, width), BF)
    return pl.pallas_call(
        ffn_kernel,
        out_shape=(part, part, jax.ShapeDtypeStruct((pages, width), F32)),
        in_specs=[smem()] + [anym()] * 8 + [vmem()] + [anym()] * 2 + [vmem()],
        out_specs=(vmem(),) * 3,
        scratch_shapes=[
            pltpu.VMEM((count, 2 * SIDE * SIDE * HD), BF),
            pltpu.VMEM((count, width), BF),
            pltpu.VMEM((count, units), BF),
            pltpu.VMEM((2, width, units), BF),
            pltpu.VMEM((units, width), BF),
            pltpu.VMEM((count // pages, pages, 512), F32),
            pltpu.SemaphoreType.DMA((40,)),
        ],
        compiler_params=params(40),
        cost_estimate=pl.CostEstimate(
            flops=6 * count * width * units, bytes_accessed=6 * width * units, transcendentals=0
        ),
    )(pos, *pieces, *pieces_t, gain, gate_up, down, pick)


def on_device(
    tokens,
    page_lengths,
    page_group,
    page_report,
    attn_gain,
    w_query,
    w_keyval,
    w_out,
    doc_gain,
    ffn_gain,
    gate_up_weight,
    w_down,
):
    count, width = tokens.shape
    pages = page_lengths.shape[1]
    grp = lax.axis_index("grp")
    page = lax.axis_index("page")
    core = page % 2
    z = (page // 2) % SIDE
    x = page // (2 * SIDE)
    pos = jnp.stack([core, grp, x, z]).astype(jnp.int32)

    out_half = w_out.shape[1] // 2
    q_half = w_query.shape[1] // 2

    def out_cols(c):
        return lax.dynamic_slice_in_dim(w_out, c * out_half, out_half, 1)

    def qkv_cols(c):
        return jnp.concatenate(
            [
                lax.dynamic_slice_in_dim(w_query, c * q_half, q_half, 1),
                lax.dynamic_slice_in_dim(w_keyval, c * HD, HD, 1),
                lax.dynamic_slice_in_dim(w_keyval, (2 + c) * HD, HD, 1),
            ],
            axis=1,
        )

    def pair_up(mine, got):
        low = jnp.where(core == 0, mine, got)
        high = jnp.where(core == 0, got, mine)
        return jnp.concatenate([low, high], axis=0)

    wo_got = swap(out_cols(1 - core))
    w_query, w_keyval, wo_got = lax.optimization_barrier((w_query, w_keyval, wo_got))
    wo = pair_up(out_cols(core), wo_got)
    wq = pair_up(qkv_cols(core), swap(qkv_cols(1 - core)))
    wo_y = lax.dynamic_slice_in_dim(wo, grp * WY, WY, 1)
    tile = (out_half - SIDE * WY) // 2
    wo_r = wo[:, SIDE * WY :]
    wq = jnp.concatenate([wq, jnp.concatenate([wo_r[:, :tile], wo_r[:, tile:]], axis=0)], axis=1)

    tok_other = swap(tokens)
    len_other = swap(page_lengths)
    gain = attn_gain[None, :]
    x_own = norm_blocks(tokens, gain)
    x_other = norm_blocks(tok_other, gain)
    seg_own = page_index(page_lengths[0], count)
    seg_other = page_index(len_other[0], count)
    seg_col = jnp.concatenate([seg_own, seg_other])[:, None]
    seg_row = jnp.stack([seg_own, seg_other])[:, None, :]
    names = jnp.arange(pages, dtype=jnp.int32)[:, None]
    members = tuple((seg[None, :] == names).astype(BF) for seg in (seg_own, seg_other))
    lens = tuple(v[0][:, None].astype(F32) for v in (page_lengths, len_other))
    slots = 2 * SIDE * SIDE
    plane = slots * pages
    labels = page_group * REPORTS + page_report[:, None]
    head_gain = jnp.pad(doc_gain, (0, slots * HD - width))
    head_gain = lax.dynamic_slice_in_dim(head_gain, page * HD, HD)[None, :]
    pick = (
        jnp.arange(plane, dtype=jnp.int32)[None, :] == page * pages + jnp.arange(pages)[:, None]
    ).astype(BF)
    early = (seg_col, seg_row, members, lens, labels, head_gain, pick, pos, ffn_gain[None, :])

    line_y = jnp.stack([wo_y, move_a(wo_y, 1), move_a(wo_y, 2), move_a(wo_y, -1)])
    line_y, wq = lax.optimization_barrier((line_y, wq))
    square = (line_y, move_b(line_y, 1), move_b(line_y, 2), move_b(line_y, -1))
    q1, q3 = move_a(wq, 1), move_a(wq, -1)
    square, q1, q3 = lax.optimization_barrier((square, q1, q3))
    q1, q2, q3 = lax.optimization_barrier((q1, move_a(wq, 2), q3))
    wo_all = lax.all_gather(arrange(pos, square), "grp", axis=0, tiled=True)
    wo_all = wo_all.reshape(SIDE, -1, WY)
    low = jnp.stack([wq, q1])
    high = jnp.stack([q2, q3])
    up = [move_b(low, 1), move_b(high, 1)]
    down = [move_b(low, -1), move_b(high, -1)]
    up[0], x_own, x_other, early = lax.optimization_barrier((up[0], x_own, x_other, early))
    far = [move_b(up[0], 1), move_b(down[1], -1)]
    pieces = [low, high] + up + far + down
    seg_col, seg_row, members, lens, labels, head_gain, pick, pos, ffn_row = early

    part = qkv_first(pos, x_own, x_other, pieces[:4] + pieces[6:], QKV_COLS)
    att = qkv_last(pos, x_own, x_other, seg_col, seg_row, part, far)
    att_in = swap(att)
    st_own, st_other, pool_own, pool_other = page_out(
        pos, tokens, tok_other, att, att_in, members, lens, wo_all, pieces
    )

    def side_by_side(mine, got):
        left = jnp.where(core == 0, mine, got)
        right = jnp.where(core == 0, got, mine)
        return jnp.concatenate([left, right], axis=1)

    vectors = side_by_side(pool_own, swap(pool_other))
    token_states = side_by_side(st_own, swap(st_other))

    blocks = page_blocks(vectors, labels, slots)
    blocks = jnp.broadcast_to(blocks[None], (SIDE,) + blocks.shape).reshape(-1, pages, 2 * HD)
    gathered = lax.all_to_all(blocks, ("grp", "page"), split_axis=0, concat_axis=0, tiled=True)
    mixed = doc_attention(pos, gathered.reshape(-1, 2 * HD), head_gain, plane)

    line = jnp.stack([mixed, move_a(mixed, 1), move_a(mixed, 2), move_a(mixed, -1)])
    pieces = (line, move_b(line, 1), move_b(line, 2), move_b(line, -1))
    pieces_t = tuple(swap(v) for v in pieces)
    own, other, states = feed_forward(
        pos, pieces, pieces_t, ffn_row, gate_up_weight, w_down, pick
    )
    got = swap(other)

    def total(*terms):
        return sum(v.astype(F32) for v in terms)

    part = [total(own[j], got[j]).astype(BF) for j in range(SIDE)]
    part = total(part[0], *(move_a(part[j], j) for j in range(1, SIDE)))
    part = [part[k].astype(BF) if k else part[k] for k in range(SIDE)]
    summed = total(part[0], *(move_b(part[k], k) for k in range(1, SIDE)))
    page_embeddings = (states + summed).astype(BF)
    return (token_states, page_embeddings)


def solution(mesh):
    in_specs = (
        P(("grp", "page"), None),
        P(("grp", "page"), None),
        P(("grp", "page"), None),
        P(("grp", "page")),
        P(),
        P("page", None),
        P("page", None),
        P("page", None),
        P(),
        P(),
        P(None, None, "page"),
        P("page", None),
    )
    out_specs = (P(("grp", "page"), None), P(("grp", "page"), None))
    return jax.shard_map(
        on_device, mesh=mesh, in_specs=in_specs, out_specs=out_specs, check_vma=False
    )
```

```python
import functools
import math

import jax
import jax.numpy as jnp
from jax import lax
from jax.experimental import pallas as pl
from jax.experimental.pallas import tpu as pltpu
from jax.sharding import PartitionSpec as P

HD = 128
REPORTS = 16
SIDE = 4
WY = 384
BF = jnp.bfloat16
F32 = jnp.float32
MIB = 1 << 20


def vmem():
    return pl.BlockSpec(memory_space=pltpu.VMEM)


def smem():
    return pl.BlockSpec(memory_space=pltpu.SMEM)


def anym():
    return pl.BlockSpec(memory_space=pl.ANY)


def params(mib):
    return pltpu.CompilerParams(vmem_limit_bytes=mib * MIB)


def chip_perm(step):
    pairs = []
    for x in range(SIDE):
        for z in range(SIDE):
            for c in range(2):
                a, b, d = step(x, z, c)
                pairs.append(((x * SIDE + z) * 2 + c, ((a % SIDE) * SIDE + b % SIDE) * 2 + d))
    return pairs


def swap(v):
    return lax.ppermute(v, "page", chip_perm(lambda x, z, c: (x, z, 1 - c)))


def move_a(v, k):
    return lax.ppermute(
        v, "page", chip_perm(lambda x, z, c: (x + k, z, c) if c == 0 else (x, z + k, c))
    )


def move_b(v, k):
    return lax.ppermute(
        v, "page", chip_perm(lambda x, z, c: (x, z + k, c) if c == 0 else (x + k, z, c))
    )


def rms_scale(values, gain):
    wide = values.astype(F32)
    return wide * lax.rsqrt(jnp.mean(wide * wide, axis=-1, keepdims=True) + 1e-06) * gain


def page_index(lengths, count):
    ends = jnp.cumsum(lengths, dtype=jnp.int32)
    position = jnp.arange(count, dtype=jnp.int32)
    return jnp.sum((position[:, None] >= ends[None, :]).astype(jnp.int32), axis=1)


def chip_at(pos, core, j, k, sign):
    shift_x = jnp.where(core == 0, sign * j, sign * k)
    shift_z = jnp.where(core == 0, sign * k, sign * j)
    return lax.rem(pos[2] + SIDE + shift_x, SIDE) * SIDE + lax.rem(pos[3] + SIDE + shift_z, SIDE)


def run_copies(copies, sems):
    started = []
    for i, (src, dst) in enumerate(copies):
        copy = pltpu.make_async_copy(src, dst, sems.at[i])
        copy.start()
        started.append(copy)
    return started


QKV_COLS = 1152
BLOCK = 256


def norm_kernel(tok, gain, out, wide_ref):
    chunk = 32
    depth = tok.shape[1] // out.shape[0]

    @pl.loop(0, tok.shape[0] // chunk)
    def _(i):
        rows = pl.ds(pl.multiple_of(i * chunk, chunk), chunk)
        wide = tok[rows, :].astype(F32)
        scale = lax.rsqrt(jnp.mean(wide * wide, axis=1, keepdims=True) + 1e-06)
        wide_ref[...] = wide * scale * gain[...]
        for n in range(out.shape[0]):
            piece = wide_ref[:, n * depth : (n + 1) * depth]
            pad = jnp.zeros((chunk, BLOCK - depth), F32)
            out[n, rows, :] = jnp.concatenate([piece, pad], axis=1).astype(BF)


def norm_blocks(tok, gain):
    count, width = tok.shape
    chips = SIDE * SIDE
    return pl.pallas_call(
        norm_kernel,
        out_shape=jax.ShapeDtypeStruct((chips, count, BLOCK), BF),
        in_specs=[vmem()] * 2,
        out_specs=vmem(),
        scratch_shapes=[pltpu.VMEM((32, width), F32)],
        compiler_params=params(24),
        cost_estimate=pl.CostEstimate(flops=0, bytes_accessed=4 * count * width, transcendentals=0),
    )(tok, gain)


def qkv_load(pos, steps, pieces, xo, xt, w, x, sems):
    cols = w.shape[1]
    depth = pieces[0].shape[1]
    tokens = xo.shape[1]
    copies = []
    for n in range(2 * len(pieces)):
        piece = pieces[n // 2].at[n % 2, :, pl.ds(0, cols)]
        copies.append((piece, w.at[pl.ds(n * BLOCK, depth), :]))
    started = run_copies(copies, sems)
    for n in range(2 * len(pieces)):
        q = chip_at(pos, pos[0], n % SIDE, steps[n // SIDE], -1)
        x[0:tokens, n * BLOCK : (n + 1) * BLOCK] = xo[q]
        x[tokens : 2 * tokens, n * BLOCK : (n + 1) * BLOCK] = xt[q]
        w[n * BLOCK + depth : (n + 1) * BLOCK, :] = jnp.zeros((BLOCK - depth, cols), BF)
    for copy in started:
        copy.wait()


QKV_TILE = 384


def qkv_first_kernel(pos, xo, xt, *refs):
    *pieces, part, w, x, sems = refs
    qkv_load(pos, (0, 1, 3), pieces, xo, xt, w, x, sems)

    @pl.loop(0, part.shape[1] // QKV_TILE)
    def _(n):
        there = pl.ds(pl.multiple_of(n * QKV_TILE, 128), QKV_TILE)
        part[:, there] = jnp.dot(x[...], w[:, there], preferred_element_type=F32)


def qkv_last_kernel(pos, xo, xt, seg_col, seg_row, part, *refs):
    *pieces, out, w, x, qkv, sems = refs
    qkv_load(pos, (2,), pieces, xo, xt, w, x, sems)

    for lo in range(0, part.shape[1], BLOCK):
        there = slice(lo, min(lo + BLOCK, part.shape[1]))
        last = jnp.dot(x[...], w[:, there], preferred_element_type=F32)
        qkv[:, there] = (part[:, there] + last).astype(BF)

    heads = out.shape[1] // HD
    tokens = xo.shape[1]

    @pl.loop(0, 2)
    def _(b):
        rows = pl.ds(pl.multiple_of(b * tokens, tokens), tokens)
        same = seg_col[rows, :] == seg_row[b]
        keys = qkv[rows, heads * HD : (heads + 1) * HD]
        values = jnp.concatenate(
            [qkv[rows, (heads + 1) * HD : (heads + 2) * HD], jnp.ones((tokens, HD), BF)], axis=1
        )
        for h in range(heads):
            query = qkv[rows, h * HD : (h + 1) * HD]
            scores = lax.dot_general(
                query, keys, (((1,), (1,)), ((), ())), preferred_element_type=F32
            ) * (math.log2(math.e) / math.sqrt(HD))
            scores = jnp.where(same, scores, -1e30)
            top = jnp.max(scores, axis=1, keepdims=True)
            weights = jnp.exp2(scores - top).astype(BF)
            mixed = jnp.dot(weights, values, preferred_element_type=F32)
            out[rows, h * HD : (h + 1) * HD] = (mixed[:, 0:HD] / mixed[:, HD : 2 * HD]).astype(BF)


def qkv_first(pos, x_own, x_other, pieces, cols):
    tokens = x_own.shape[1]
    return pl.pallas_call(
        qkv_first_kernel,
        out_shape=jax.ShapeDtypeStruct((2 * tokens, cols), F32),
        in_specs=[smem()] + [vmem()] * 2 + [anym()] * 6,
        out_specs=vmem(),
        scratch_shapes=[
            pltpu.VMEM((12 * BLOCK, cols), BF),
            pltpu.VMEM((2 * tokens, 12 * BLOCK), BF),
            pltpu.SemaphoreType.DMA((12,)),
        ],
        compiler_params=params(40),
        cost_estimate=pl.CostEstimate(
            flops=4 * tokens * 12 * BLOCK * cols, bytes_accessed=24 * BLOCK * cols, transcendentals=0
        ),
    )(pos, x_own, x_other, *pieces)


def qkv_last(pos, x_own, x_other, seg_col, seg_row, part, pieces):
    tokens = x_own.shape[1]
    cols = part.shape[1]
    return pl.pallas_call(
        qkv_last_kernel,
        out_shape=jax.ShapeDtypeStruct((2 * tokens, cols - 2 * HD), BF),
        in_specs=[smem()] + [vmem()] * 5 + [anym()] * 2,
        out_specs=vmem(),
        scratch_shapes=[
            pltpu.VMEM((4 * BLOCK, cols), BF),
            pltpu.VMEM((2 * tokens, 4 * BLOCK), BF),
            pltpu.VMEM((2 * tokens, cols), BF),
            pltpu.SemaphoreType.DMA((4,)),
        ],
        compiler_params=params(40),
        cost_estimate=pl.CostEstimate(
            flops=4 * tokens * 8 * BLOCK * cols, bytes_accessed=24 * BLOCK * cols, transcendentals=0
        ),
    )(pos, x_own, x_other, seg_col, seg_row, part, *pieces)


def arrange_kernel(pos, t, b1, b2, b3, out):
    for k, piece in enumerate((t, b1, b2, b3)):
        for j in range(SIDE):
            out[chip_at(pos, pos[0], j, k, -1)] = piece[j]


def arrange(pos, pieces):
    n, rows, cols = pieces[0].shape
    return pl.pallas_call(
        arrange_kernel,
        out_shape=jax.ShapeDtypeStruct((SIDE * n, rows, cols), BF),
        in_specs=[smem()] + [vmem()] * 4,
        out_specs=vmem(),
        compiler_params=params(16),
        cost_estimate=pl.CostEstimate(
            flops=0, bytes_accessed=4 * SIDE * n * rows * cols, transcendentals=0
        ),
    )(pos, *pieces)


def out_kernel(
    pos, tok_own, tok_other, att, att_in, member, member_t, inv, inv_t, w_all, *refs
):
    pieces, refs = refs[: 2 * SIDE], refs[2 * SIDE :]
    st_own, st_other, pool_own, pool_other, w, rest, full, sems = refs
    core = pos[0]
    wy = w_all.shape[2]
    depth = pieces[0].shape[1] // 2
    tile = rest.shape[1] // 2
    chips = SIDE * SIDE
    copies = []
    rows = [
        pl.ds(pl.multiple_of(chip_at(pos, core, n % SIDE, n // SIDE, -1) * depth, 16), depth)
        for n in range(chips)
    ]
    for i in range(SIDE):
        copies.append((w_all.at[i], w.at[i]))
    for n in range(chips):
        for t in range(2):
            copies.append(
                (
                    pieces[n // 2].at[n % 2, pl.ds(t * depth, depth), pl.ds(QKV_COLS, tile)],
                    rest.at[rows[n], pl.ds(t * tile, tile)],
                )
            )
    started = run_copies(copies, sems)
    tokens = tok_own.shape[0]
    half = att.shape[1]
    mine = pl.ds(pl.multiple_of(core * half, 128), half)
    theirs = pl.ds(pl.multiple_of((1 - core) * half, 128), half)
    full[:, mine] = att[...]
    full[0:tokens, theirs] = att_in[tokens : 2 * tokens, :]
    full[tokens : 2 * tokens, theirs] = att_in[0:tokens, :]
    width = st_own.shape[1]

    def columns(lo, n, weight):
        cols = slice(lo, lo + n)
        there = pl.ds(pl.multiple_of(core * width + lo, 128), n)
        projected = jnp.dot(full[...], weight, preferred_element_type=F32)
        for first, tok, st, mem, ratio, pool in (
            (0, tok_own, st_own, member, inv, pool_own),
            (tokens, tok_other, st_other, member_t, inv_t, pool_other),
        ):
            states = (tok[:, there].astype(F32) + projected[first : first + tokens]).astype(BF)
            st[:, cols] = states
            pool[:, cols] = (
                jnp.dot(mem[...], states, preferred_element_type=F32) / ratio[...]
            ).astype(BF)

    for i in range(SIDE):
        started[i].wait()
        columns(i * wy, wy, w[i])
    for copy in started[SIDE:]:
        copy.wait()
    columns(SIDE * wy, 2 * tile, rest[...])


def page_out(pos, tok_own, tok_other, att, att_in, members, lens, w_all, pieces):
    tokens, width = tok_own.shape
    width = width // 2
    rows, wy = w_all.shape[1:]
    pages = members[0].shape[0]
    st = jax.ShapeDtypeStruct((tokens, width), BF)
    pool = jax.ShapeDtypeStruct((pages, width), BF)
    return pl.pallas_call(
        out_kernel,
        out_shape=(st, st, pool, pool),
        in_specs=[smem()] + [vmem()] * 8 + [anym()] * 9,
        out_specs=(vmem(),) * 4,
        scratch_shapes=[
            pltpu.VMEM((SIDE, rows, wy), BF),
            pltpu.VMEM((rows, width - SIDE * wy), BF),
            pltpu.VMEM((2 * tokens, rows), BF),
            pltpu.SemaphoreType.DMA((SIDE + 2 * SIDE * SIDE,)),
        ],
        compiler_params=params(40),
        cost_estimate=pl.CostEstimate(
            flops=2 * 2 * tokens * width * rows, bytes_accessed=2 * width * rows, transcendentals=0
        ),
    )(pos, tok_own, tok_other, att, att_in, *members, *lens, w_all, *pieces)


def block_kernel(vec, label, out):
    pages, width = vec.shape
    wide = vec[...].astype(F32)
    scale = lax.rsqrt(jnp.mean(wide * wide, axis=1, keepdims=True) + 1e-06)
    high = scale.astype(BF)
    low = (scale - high.astype(F32)).astype(BF)
    lane = lax.broadcasted_iota(jnp.int32, (pages, HD), 1)
    side = jnp.where(lane == 0, high.astype(F32), jnp.where(lane == 1, low.astype(F32), 0.0))
    side = jnp.where(lane == 2, label[...].astype(F32), side).astype(BF)
    for h in range(width // HD):
        out[h, :, 0:HD] = vec[:, h * HD : (h + 1) * HD]
        out[h, :, HD : 2 * HD] = side
    for h in range(width // HD, out.shape[0]):
        out[h] = jnp.zeros((pages, 2 * HD), BF)


def page_blocks(vectors, labels, slots):
    return pl.pallas_call(
        block_kernel,
        out_shape=jax.ShapeDtypeStruct((slots, vectors.shape[0], 2 * HD), BF),
        in_specs=[vmem()] * 2,
        out_specs=vmem(),
        compiler_params=params(16),
    )(vectors, labels)


def doc_kernel(pos, rows, gain, out, keys_ref):
    count = out.shape[0]
    every = rows.shape[0]
    start = pl.multiple_of(pos[1] * count, count)
    mine = pl.ds(start, count)
    side = rows[:, HD : 2 * HD].astype(F32)
    scale = side[:, 0:1] + side[:, 1:2]
    keys = (rows[:, 0:HD].astype(F32) * scale * gain[...]).astype(BF)
    keys_ref[...] = keys
    query = keys_ref[mine, :]
    pick = (lax.broadcasted_iota(jnp.int32, (8, HD), 1) == 2).astype(BF)
    label_row = lax.dot_general(
        pick, rows[:, HD : 2 * HD], (((1,), (1,)), ((), ())), preferred_element_type=F32
    )[0:1, :]
    label_col = rows[mine, HD : 2 * HD].astype(F32)[:, 2:3]
    scores = lax.dot_general(
        query, keys, (((1,), (1,)), ((), ())), preferred_element_type=F32
    ) * (math.log2(math.e) / HD)
    scores = jnp.where(label_col == label_row, scores, -1e30)
    top = jnp.max(scores, axis=1, keepdims=True)
    e = jnp.exp2(scores - top)
    weights = (e * (1.0 / jnp.sum(e, axis=1, keepdims=True))).astype(BF)
    context = jnp.dot(weights, keys, preferred_element_type=F32)
    out[...] = (rows[mine, 0:HD].astype(F32) + context).astype(BF)


def doc_attention(pos, rows, gain, count):
    return pl.pallas_call(
        doc_kernel,
        out_shape=jax.ShapeDtypeStruct((count, HD), BF),
        in_specs=[smem()] + [vmem()] * 2,
        out_specs=vmem(),
        scratch_shapes=[pltpu.VMEM((rows.shape[0], HD), BF)],
        compiler_params=params(24),
    )(pos, rows, gain)


def ffn_kernel(
    pos, t, b1, b2, b3, tt, c1, c2, c3, gain, wgu, wd, pick,
    own, other, states, x, mixed, hidden, acc, sems,
):
    core = pos[0]
    width = gain.shape[1]
    units = hidden.shape[1]
    half = units // 2
    copies = []
    for side, pieces in ((core, (t, b1, b2, b3)), (1 - core, (tt, c1, c2, c3))):
        for k, piece in enumerate(pieces):
            for j in range(SIDE):
                head = chip_at(pos, side, j, k, -1) * 2 + side
                copies.append((piece.at[j], x.at[:, pl.ds(pl.multiple_of(head * HD, HD), HD)]))
    for copy in run_copies(copies, sems):
        copy.wait()
    chunk = 32

    @pl.loop(0, x.shape[0] // chunk)
    def _(i):
        rows = pl.ds(pl.multiple_of(i * chunk, chunk), chunk)
        wide = x[rows, 0:width].astype(F32)
        scale = lax.rsqrt(jnp.mean(wide * wide, axis=1, keepdims=True) + 1e-06)
        mixed[rows, :] = (wide * scale * gain[...]).astype(BF)

    for n in range(2):
        cols = slice(n * half, (n + 1) * half)
        gate = jnp.dot(mixed[...], wgu[0, :, cols], preferred_element_type=F32)
        up = jnp.dot(mixed[...], wgu[1, :, cols], preferred_element_type=F32)
        hidden[:, cols] = (gate * jax.nn.sigmoid(gate) * up).astype(BF)
    tile = 512

    @pl.loop(0, width // tile)
    def _(n):
        cols = pl.ds(pl.multiple_of(n * tile, 128), tile)
        part = jnp.dot(hidden[...], wd[:, cols], preferred_element_type=F32)
        acc[...] = part.reshape(acc.shape)
        for k in range(SIDE):
            for j in range(SIDE):
                own[j, k, :, cols] = acc[chip_at(pos, core, j, k, 1) * 2 + core].astype(BF)
                other[j, k, :, cols] = acc[chip_at(pos, 1 - core, j, k, 1) * 2 + 1 - core].astype(BF)
        states[:, cols] = jnp.dot(pick[...], x[:, cols], preferred_element_type=F32)


def load_kernel(src, out, sem):
    copy = pltpu.make_async_copy(src, out, sem)
    copy.start()
    copy.wait()


def load_weights(weights):
    return pl.pallas_call(
        load_kernel,
        out_shape=jax.ShapeDtypeStruct(weights.shape, weights.dtype),
        in_specs=[anym()],
        out_specs=vmem(),
        scratch_shapes=[pltpu.SemaphoreType.DMA],
        compiler_params=params(12),
        cost_estimate=pl.CostEstimate(flops=0, bytes_accessed=2 * weights.size, transcendentals=0),
    )(weights)


def feed_forward(pos, pieces, pieces_t, gain, gate_up, down, pick):
    width = gain.shape[1]
    units = down.shape[0]
    pages, count = pick.shape
    part = jax.ShapeDtypeStruct((SIDE, SIDE, pages, width), BF)
    return pl.pallas_call(
        ffn_kernel,
        out_shape=(part, part, jax.ShapeDtypeStruct((pages, width), F32)),
        in_specs=[smem()] + [anym()] * 8 + [vmem()] * 4,
        out_specs=(vmem(),) * 3,
        scratch_shapes=[
            pltpu.VMEM((count, 2 * SIDE * SIDE * HD), BF),
            pltpu.VMEM((count, width), BF),
            pltpu.VMEM((count, units), BF),
            pltpu.VMEM((count // pages, pages, 512), F32),
            pltpu.SemaphoreType.DMA((40,)),
        ],
        compiler_params=params(12),
        cost_estimate=pl.CostEstimate(
            flops=6 * count * width * units, bytes_accessed=6 * width * units, transcendentals=0
        ),
    )(pos, *pieces, *pieces_t, gain, gate_up, down, pick)


def on_device(
    tokens,
    page_lengths,
    page_group,
    page_report,
    attn_gain,
    w_query,
    w_keyval,
    w_out,
    doc_gain,
    ffn_gain,
    gate_up_weight,
    w_down,
):
    count, width = tokens.shape
    pages = page_lengths.shape[1]
    grp = lax.axis_index("grp")
    page = lax.axis_index("page")
    core = page % 2
    z = (page // 2) % SIDE
    x = page // (2 * SIDE)
    pos = jnp.stack([core, grp, x, z]).astype(jnp.int32)

    out_half = w_out.shape[1] // 2
    q_half = w_query.shape[1] // 2

    def out_cols(c):
        return lax.dynamic_slice_in_dim(w_out, c * out_half, out_half, 1)

    def qkv_cols(c):
        return jnp.concatenate(
            [
                lax.dynamic_slice_in_dim(w_query, c * q_half, q_half, 1),
                lax.dynamic_slice_in_dim(w_keyval, c * HD, HD, 1),
                lax.dynamic_slice_in_dim(w_keyval, (2 + c) * HD, HD, 1),
            ],
            axis=1,
        )

    def pair_up(mine, got):
        low = jnp.where(core == 0, mine, got)
        high = jnp.where(core == 0, got, mine)
        return jnp.concatenate([low, high], axis=0)

    wo_got = swap(out_cols(1 - core))
    w_query, w_keyval, wo_got = lax.optimization_barrier((w_query, w_keyval, wo_got))
    wo = pair_up(out_cols(core), wo_got)
    wq = pair_up(qkv_cols(core), swap(qkv_cols(1 - core)))
    wo_y = lax.dynamic_slice_in_dim(wo, grp * WY, WY, 1)
    tile = (out_half - SIDE * WY) // 2
    wo_r = wo[:, SIDE * WY :]
    wq = jnp.concatenate([wq, jnp.concatenate([wo_r[:, :tile], wo_r[:, tile:]], axis=0)], axis=1)

    tok_other = swap(tokens)
    len_other = swap(page_lengths)
    gain = attn_gain[None, :]
    x_own = norm_blocks(tokens, gain)
    x_other = norm_blocks(tok_other, gain)
    seg_own = page_index(page_lengths[0], count)
    seg_other = page_index(len_other[0], count)
    seg_col = jnp.concatenate([seg_own, seg_other])[:, None]
    seg_row = jnp.stack([seg_own, seg_other])[:, None, :]
    names = jnp.arange(pages, dtype=jnp.int32)[:, None]
    members = tuple((seg[None, :] == names).astype(BF) for seg in (seg_own, seg_other))
    lens = tuple(v[0][:, None].astype(F32) for v in (page_lengths, len_other))
    slots = 2 * SIDE * SIDE
    plane = slots * pages
    labels = page_group * REPORTS + page_report[:, None]
    head_gain = jnp.pad(doc_gain, (0, slots * HD - width))
    head_gain = lax.dynamic_slice_in_dim(head_gain, page * HD, HD)[None, :]
    pick = (
        jnp.arange(plane, dtype=jnp.int32)[None, :] == page * pages + jnp.arange(pages)[:, None]
    ).astype(BF)
    early = (seg_col, seg_row, members, lens, labels, head_gain, pick, pos, ffn_gain[None, :])

    line_y = jnp.stack([wo_y, move_a(wo_y, 1), move_a(wo_y, 2), move_a(wo_y, -1)])
    line_y, wq = lax.optimization_barrier((line_y, wq))
    square = (line_y, move_b(line_y, 1), move_b(line_y, 2), move_b(line_y, -1))
    q1, q3 = move_a(wq, 1), move_a(wq, -1)
    square, q1, q3 = lax.optimization_barrier((square, q1, q3))
    q1, q2, q3 = lax.optimization_barrier((q1, move_a(wq, 2), q3))
    wo_all = lax.all_gather(arrange(pos, square), "grp", axis=0, tiled=True)
    wo_all = wo_all.reshape(SIDE, -1, WY)
    low = jnp.stack([wq, q1])
    high = jnp.stack([q2, q3])
    up = [move_b(low, 1), move_b(high, 1)]
    down = [move_b(low, -1), move_b(high, -1)]
    up[0], x_own, x_other, early = lax.optimization_barrier((up[0], x_own, x_other, early))
    far = [move_b(up[0], 1), move_b(down[1], -1)]
    pieces = [low, high] + up + far + down
    seg_col, seg_row, members, lens, labels, head_gain, pick, pos, ffn_row = early

    part = qkv_first(pos, x_own, x_other, pieces[:4] + pieces[6:], QKV_COLS)
    att = qkv_last(pos, x_own, x_other, seg_col, seg_row, part, far)
    att_in = swap(att)
    st_own, st_other, pool_own, pool_other = page_out(
        pos, tokens, tok_other, att, att_in, members, lens, wo_all, pieces
    )

    def side_by_side(mine, got):
        left = jnp.where(core == 0, mine, got)
        right = jnp.where(core == 0, got, mine)
        return jnp.concatenate([left, right], axis=1)

    vectors = side_by_side(pool_own, swap(pool_other))
    token_states = side_by_side(st_own, swap(st_other))

    blocks = page_blocks(vectors, labels, slots)
    blocks = jnp.broadcast_to(blocks[None], (SIDE,) + blocks.shape).reshape(-1, pages, 2 * HD)
    gathered = lax.all_to_all(blocks, ("grp", "page"), split_axis=0, concat_axis=0, tiled=True)
    gathered, gate_up_weight = lax.optimization_barrier((gathered, gate_up_weight))
    gate_up_weight = load_weights(gate_up_weight)
    mixed = doc_attention(pos, gathered.reshape(-1, 2 * HD), head_gain, plane)

    line = jnp.stack([mixed, move_a(mixed, 1), move_a(mixed, 2), move_a(mixed, -1)])
    line, gate_up_weight = lax.optimization_barrier((line, gate_up_weight))
    pieces = (line, move_b(line, 1), move_b(line, 2), move_b(line, -1))
    pieces_t = tuple(swap(v) for v in pieces)
    own, other, states = feed_forward(
        pos, pieces, pieces_t, ffn_row, gate_up_weight, w_down, pick
    )
    got = swap(other)

    def total(*terms):
        return sum(v.astype(F32) for v in terms)

    part = [total(own[j], got[j]).astype(BF) for j in range(SIDE)]
    part = total(part[0], *(move_a(part[j], j) for j in range(1, SIDE)))
    part = [part[k].astype(BF) if k else part[k] for k in range(SIDE)]
    summed = total(part[0], *(move_b(part[k], k) for k in range(1, SIDE)))
    page_embeddings = (states + summed).astype(BF)
    return (token_states, page_embeddings)


def solution(mesh):
    in_specs = (
        P(("grp", "page"), None),
        P(("grp", "page"), None),
        P(("grp", "page"), None),
        P(("grp", "page")),
        P(),
        P("page", None),
        P("page", None),
        P("page", None),
        P(),
        P(),
        P(None, None, "page"),
        P("page", None),
    )
    out_specs = (P(("grp", "page"), None), P(("grp", "page"), None))
    return jax.shard_map(
        on_device, mesh=mesh, in_specs=in_specs, out_specs=out_specs, check_vma=False
    )
```

```python
import functools
import math

import jax
import jax.numpy as jnp
from jax import lax
from jax.experimental import pallas as pl
from jax.experimental.pallas import tpu as pltpu
from jax.sharding import PartitionSpec as P

HD = 128
REPORTS = 16
SIDE = 4
WY = 384
BF = jnp.bfloat16
F32 = jnp.float32
MIB = 1 << 20


def vmem():
    return pl.BlockSpec(memory_space=pltpu.VMEM)


def smem():
    return pl.BlockSpec(memory_space=pltpu.SMEM)


def anym():
    return pl.BlockSpec(memory_space=pl.ANY)


def params(mib):
    return pltpu.CompilerParams(vmem_limit_bytes=mib * MIB)


def chip_perm(step):
    pairs = []
    for x in range(SIDE):
        for z in range(SIDE):
            for c in range(2):
                a, b, d = step(x, z, c)
                pairs.append(((x * SIDE + z) * 2 + c, ((a % SIDE) * SIDE + b % SIDE) * 2 + d))
    return pairs


def swap(v):
    return lax.ppermute(v, "page", chip_perm(lambda x, z, c: (x, z, 1 - c)))


def move_a(v, k):
    return lax.ppermute(
        v, "page", chip_perm(lambda x, z, c: (x + k, z, c) if c == 0 else (x, z + k, c))
    )


def move_b(v, k):
    return lax.ppermute(
        v, "page", chip_perm(lambda x, z, c: (x, z + k, c) if c == 0 else (x + k, z, c))
    )


def rms_scale(values, gain):
    wide = values.astype(F32)
    return wide * lax.rsqrt(jnp.mean(wide * wide, axis=-1, keepdims=True) + 1e-06) * gain


def page_index(lengths, count):
    ends = jnp.cumsum(lengths, dtype=jnp.int32)
    position = jnp.arange(count, dtype=jnp.int32)
    return jnp.sum((position[:, None] >= ends[None, :]).astype(jnp.int32), axis=1)


def chip_at(pos, core, j, k, sign):
    shift_x = jnp.where(core == 0, sign * j, sign * k)
    shift_z = jnp.where(core == 0, sign * k, sign * j)
    return lax.rem(pos[2] + SIDE + shift_x, SIDE) * SIDE + lax.rem(pos[3] + SIDE + shift_z, SIDE)


def run_copies(copies, sems):
    started = []
    for i, (src, dst) in enumerate(copies):
        copy = pltpu.make_async_copy(src, dst, sems.at[i])
        copy.start()
        started.append(copy)
    return started


QKV_COLS = 1152
BLOCK = 256


def norm_kernel(tok, gain, out, wide_ref):
    chunk = 32
    depth = tok.shape[1] // out.shape[0]

    @pl.loop(0, tok.shape[0] // chunk)
    def _(i):
        rows = pl.ds(pl.multiple_of(i * chunk, chunk), chunk)
        wide = tok[rows, :].astype(F32)
        scale = lax.rsqrt(jnp.mean(wide * wide, axis=1, keepdims=True) + 1e-06)
        wide_ref[...] = wide * scale * gain[...]
        for n in range(out.shape[0]):
            piece = wide_ref[:, n * depth : (n + 1) * depth]
            pad = jnp.zeros((chunk, BLOCK - depth), F32)
            out[n, rows, :] = jnp.concatenate([piece, pad], axis=1).astype(BF)


def norm_blocks(tok, gain):
    count, width = tok.shape
    chips = SIDE * SIDE
    return pl.pallas_call(
        norm_kernel,
        out_shape=jax.ShapeDtypeStruct((chips, count, BLOCK), BF),
        in_specs=[vmem()] * 2,
        out_specs=vmem(),
        scratch_shapes=[pltpu.VMEM((32, width), F32)],
        compiler_params=params(24),
        cost_estimate=pl.CostEstimate(flops=0, bytes_accessed=4 * count * width, transcendentals=0),
    )(tok, gain)


def qkv_load(pos, steps, pieces, xo, xt, w, x, sems):
    cols = w.shape[1]
    depth = pieces[0].shape[1]
    tokens = xo.shape[1]
    copies = []
    for n in range(2 * len(pieces)):
        piece = pieces[n // 2].at[n % 2, :, pl.ds(0, cols)]
        copies.append((piece, w.at[pl.ds(n * BLOCK, depth), :]))
    started = run_copies(copies, sems)
    for n in range(2 * len(pieces)):
        q = chip_at(pos, pos[0], n % SIDE, steps[n // SIDE], -1)
        x[0:tokens, n * BLOCK : (n + 1) * BLOCK] = xo[q]
        x[tokens : 2 * tokens, n * BLOCK : (n + 1) * BLOCK] = xt[q]
        w[n * BLOCK + depth : (n + 1) * BLOCK, :] = jnp.zeros((BLOCK - depth, cols), BF)
    for copy in started:
        copy.wait()


QKV_TILE = 384


def qkv_first_kernel(pos, xo, xt, *refs):
    *pieces, part, w, x, sems = refs
    qkv_load(pos, (0, 1, 3), pieces, xo, xt, w, x, sems)

    @pl.loop(0, part.shape[1] // QKV_TILE)
    def _(n):
        there = pl.ds(pl.multiple_of(n * QKV_TILE, 128), QKV_TILE)
        part[:, there] = jnp.dot(x[...], w[:, there], preferred_element_type=F32)


def qkv_last_kernel(pos, xo, xt, seg_col, seg_row, part, *refs):
    *pieces, out, w, x, qkv, sems = refs
    qkv_load(pos, (2,), pieces, xo, xt, w, x, sems)

    for lo in range(0, part.shape[1], BLOCK):
        there = slice(lo, min(lo + BLOCK, part.shape[1]))
        last = jnp.dot(x[...], w[:, there], preferred_element_type=F32)
        qkv[:, there] = (part[:, there] + last).astype(BF)

    heads = out.shape[1] // HD
    tokens = xo.shape[1]

    @pl.loop(0, 2)
    def _(b):
        rows = pl.ds(pl.multiple_of(b * tokens, tokens), tokens)
        same = seg_col[rows, :] == seg_row[b]
        keys = qkv[rows, heads * HD : (heads + 1) * HD]
        values = jnp.concatenate(
            [qkv[rows, (heads + 1) * HD : (heads + 2) * HD], jnp.ones((tokens, HD), BF)], axis=1
        )
        for h in range(heads):
            query = qkv[rows, h * HD : (h + 1) * HD]
            scores = lax.dot_general(
                query, keys, (((1,), (1,)), ((), ())), preferred_element_type=F32
            ) * (math.log2(math.e) / math.sqrt(HD))
            scores = jnp.where(same, scores, -1e30)
            top = jnp.max(scores, axis=1, keepdims=True)
            weights = jnp.exp2(scores - top).astype(BF)
            mixed = jnp.dot(weights, values, preferred_element_type=F32)
            out[rows, h * HD : (h + 1) * HD] = (mixed[:, 0:HD] / mixed[:, HD : 2 * HD]).astype(BF)


def qkv_first(pos, x_own, x_other, pieces, cols):
    tokens = x_own.shape[1]
    return pl.pallas_call(
        qkv_first_kernel,
        out_shape=jax.ShapeDtypeStruct((2 * tokens, cols), F32),
        in_specs=[smem()] + [vmem()] * 2 + [anym()] * 6,
        out_specs=vmem(),
        scratch_shapes=[
            pltpu.VMEM((12 * BLOCK, cols), BF),
            pltpu.VMEM((2 * tokens, 12 * BLOCK), BF),
            pltpu.SemaphoreType.DMA((12,)),
        ],
        compiler_params=params(40),
        cost_estimate=pl.CostEstimate(
            flops=4 * tokens * 12 * BLOCK * cols, bytes_accessed=24 * BLOCK * cols, transcendentals=0
        ),
    )(pos, x_own, x_other, *pieces)


def qkv_last(pos, x_own, x_other, seg_col, seg_row, part, pieces):
    tokens = x_own.shape[1]
    cols = part.shape[1]
    return pl.pallas_call(
        qkv_last_kernel,
        out_shape=jax.ShapeDtypeStruct((2 * tokens, cols - 2 * HD), BF),
        in_specs=[smem()] + [vmem()] * 5 + [anym()] * 2,
        out_specs=vmem(),
        scratch_shapes=[
            pltpu.VMEM((4 * BLOCK, cols), BF),
            pltpu.VMEM((2 * tokens, 4 * BLOCK), BF),
            pltpu.VMEM((2 * tokens, cols), BF),
            pltpu.SemaphoreType.DMA((4,)),
        ],
        compiler_params=params(40),
        cost_estimate=pl.CostEstimate(
            flops=4 * tokens * 8 * BLOCK * cols, bytes_accessed=24 * BLOCK * cols, transcendentals=0
        ),
    )(pos, x_own, x_other, seg_col, seg_row, part, *pieces)


def arrange_kernel(pos, t, b1, b2, b3, out):
    for k, piece in enumerate((t, b1, b2, b3)):
        for j in range(SIDE):
            out[chip_at(pos, pos[0], j, k, -1)] = piece[j]


def arrange(pos, pieces):
    n, rows, cols = pieces[0].shape
    return pl.pallas_call(
        arrange_kernel,
        out_shape=jax.ShapeDtypeStruct((SIDE * n, rows, cols), BF),
        in_specs=[smem()] + [vmem()] * 4,
        out_specs=vmem(),
        compiler_params=params(16),
        cost_estimate=pl.CostEstimate(
            flops=0, bytes_accessed=4 * SIDE * n * rows * cols, transcendentals=0
        ),
    )(pos, *pieces)


def out_kernel(
    pos, tok_own, tok_other, att, att_in, member, member_t, inv, inv_t, w_all, *refs
):
    pieces, refs = refs[: 2 * SIDE], refs[2 * SIDE :]
    st_own, st_other, pool_own, pool_other, w, rest, full, sems = refs
    core = pos[0]
    wy = w_all.shape[2]
    depth = pieces[0].shape[1] // 2
    tile = rest.shape[1] // 2
    chips = SIDE * SIDE
    copies = []
    rows = [
        pl.ds(pl.multiple_of(chip_at(pos, core, n % SIDE, n // SIDE, -1) * depth, 16), depth)
        for n in range(chips)
    ]
    for i in range(SIDE):
        copies.append((w_all.at[i], w.at[i]))
    for n in range(chips):
        for t in range(2):
            copies.append(
                (
                    pieces[n // 2].at[n % 2, pl.ds(t * depth, depth), pl.ds(QKV_COLS, tile)],
                    rest.at[rows[n], pl.ds(t * tile, tile)],
                )
            )
    started = run_copies(copies, sems)
    tokens = tok_own.shape[0]
    half = att.shape[1]
    mine = pl.ds(pl.multiple_of(core * half, 128), half)
    theirs = pl.ds(pl.multiple_of((1 - core) * half, 128), half)
    full[:, mine] = att[...]
    full[0:tokens, theirs] = att_in[tokens : 2 * tokens, :]
    full[tokens : 2 * tokens, theirs] = att_in[0:tokens, :]
    width = st_own.shape[1]

    def columns(lo, n, weight):
        cols = slice(lo, lo + n)
        there = pl.ds(pl.multiple_of(core * width + lo, 128), n)
        projected = jnp.dot(full[...], weight, preferred_element_type=F32)
        for first, tok, st, mem, ratio, pool in (
            (0, tok_own, st_own, member, inv, pool_own),
            (tokens, tok_other, st_other, member_t, inv_t, pool_other),
        ):
            states = (tok[:, there].astype(F32) + projected[first : first + tokens]).astype(BF)
            st[:, cols] = states
            pool[:, cols] = (
                jnp.dot(mem[...], states, preferred_element_type=F32) / ratio[...]
            ).astype(BF)

    for i in range(SIDE):
        started[i].wait()
        columns(i * wy, wy, w[i])
    for copy in started[SIDE:]:
        copy.wait()
    columns(SIDE * wy, 2 * tile, rest[...])


def page_out(pos, tok_own, tok_other, att, att_in, members, lens, w_all, pieces):
    tokens, width = tok_own.shape
    width = width // 2
    rows, wy = w_all.shape[1:]
    pages = members[0].shape[0]
    st = jax.ShapeDtypeStruct((tokens, width), BF)
    pool = jax.ShapeDtypeStruct((pages, width), BF)
    return pl.pallas_call(
        out_kernel,
        out_shape=(st, st, pool, pool),
        in_specs=[smem()] + [vmem()] * 8 + [anym()] * 9,
        out_specs=(vmem(),) * 4,
        scratch_shapes=[
            pltpu.VMEM((SIDE, rows, wy), BF),
            pltpu.VMEM((rows, width - SIDE * wy), BF),
            pltpu.VMEM((2 * tokens, rows), BF),
            pltpu.SemaphoreType.DMA((SIDE + 2 * SIDE * SIDE,)),
        ],
        compiler_params=params(40),
        cost_estimate=pl.CostEstimate(
            flops=2 * 2 * tokens * width * rows, bytes_accessed=2 * width * rows, transcendentals=0
        ),
    )(pos, tok_own, tok_other, att, att_in, *members, *lens, w_all, *pieces)


def block_kernel(vec, label, out):
    pages, width = vec.shape
    wide = vec[...].astype(F32)
    scale = lax.rsqrt(jnp.mean(wide * wide, axis=1, keepdims=True) + 1e-06)
    high = scale.astype(BF)
    low = (scale - high.astype(F32)).astype(BF)
    lane = lax.broadcasted_iota(jnp.int32, (pages, HD), 1)
    side = jnp.where(lane == 0, high.astype(F32), jnp.where(lane == 1, low.astype(F32), 0.0))
    side = jnp.where(lane == 2, label[...].astype(F32), side).astype(BF)
    for h in range(width // HD):
        out[h, :, 0:HD] = vec[:, h * HD : (h + 1) * HD]
        out[h, :, HD : 2 * HD] = side
    for h in range(width // HD, out.shape[0]):
        out[h] = jnp.zeros((pages, 2 * HD), BF)


def page_blocks(vectors, labels, slots):
    return pl.pallas_call(
        block_kernel,
        out_shape=jax.ShapeDtypeStruct((slots, vectors.shape[0], 2 * HD), BF),
        in_specs=[vmem()] * 2,
        out_specs=vmem(),
        compiler_params=params(16),
    )(vectors, labels)


def doc_kernel(pos, rows, gain, out, keys_ref):
    count = out.shape[0]
    every = rows.shape[0]
    start = pl.multiple_of(pos[1] * count, count)
    mine = pl.ds(start, count)
    side = rows[:, HD : 2 * HD].astype(F32)
    scale = side[:, 0:1] + side[:, 1:2]
    keys = (rows[:, 0:HD].astype(F32) * scale * gain[...]).astype(BF)
    keys_ref[...] = keys
    query = keys_ref[mine, :]
    pick = (lax.broadcasted_iota(jnp.int32, (8, HD), 1) == 2).astype(BF)
    label_row = lax.dot_general(
        pick, rows[:, HD : 2 * HD], (((1,), (1,)), ((), ())), preferred_element_type=F32
    )[0:1, :]
    label_col = rows[mine, HD : 2 * HD].astype(F32)[:, 2:3]
    scores = lax.dot_general(
        query, keys, (((1,), (1,)), ((), ())), preferred_element_type=F32
    ) * (math.log2(math.e) / HD)
    scores = jnp.where(label_col == label_row, scores, -1e30)
    top = jnp.max(scores, axis=1, keepdims=True)
    e = jnp.exp2(scores - top)
    weights = (e * (1.0 / jnp.sum(e, axis=1, keepdims=True))).astype(BF)
    context = jnp.dot(weights, keys, preferred_element_type=F32)
    out[...] = (rows[mine, 0:HD].astype(F32) + context).astype(BF)


def doc_attention(pos, rows, gain, count):
    return pl.pallas_call(
        doc_kernel,
        out_shape=jax.ShapeDtypeStruct((count, HD), BF),
        in_specs=[smem()] + [vmem()] * 2,
        out_specs=vmem(),
        scratch_shapes=[pltpu.VMEM((rows.shape[0], HD), BF)],
        compiler_params=params(24),
    )(pos, rows, gain)


def ffn_kernel(
    pos, t, b1, b2, b3, tt, c1, c2, c3, gain, wgu, wd, pick,
    own, other, states, x, mixed, hidden, acc, sems,
):
    core = pos[0]
    width = gain.shape[1]
    units = hidden.shape[1]
    half = units // 2
    copies = []
    for side, pieces in ((core, (t, b1, b2, b3)), (1 - core, (tt, c1, c2, c3))):
        for k, piece in enumerate(pieces):
            for j in range(SIDE):
                head = chip_at(pos, side, j, k, -1) * 2 + side
                copies.append((piece.at[j], x.at[:, pl.ds(pl.multiple_of(head * HD, HD), HD)]))
    for copy in run_copies(copies, sems):
        copy.wait()
    chunk = 32

    @pl.loop(0, x.shape[0] // chunk)
    def _(i):
        rows = pl.ds(pl.multiple_of(i * chunk, chunk), chunk)
        wide = x[rows, 0:width].astype(F32)
        scale = lax.rsqrt(jnp.mean(wide * wide, axis=1, keepdims=True) + 1e-06)
        mixed[rows, :] = (wide * scale * gain[...]).astype(BF)

    for n in range(2):
        cols = slice(n * half, (n + 1) * half)
        gate = jnp.dot(mixed[...], wgu[0, :, cols], preferred_element_type=F32)
        up = jnp.dot(mixed[...], wgu[1, :, cols], preferred_element_type=F32)
        hidden[:, cols] = (gate * jax.nn.sigmoid(gate) * up).astype(BF)
    tile = 512

    @pl.loop(0, width // tile)
    def _(n):
        cols = pl.ds(pl.multiple_of(n * tile, 128), tile)
        part = jnp.dot(hidden[...], wd[:, cols], preferred_element_type=F32)
        acc[...] = part.reshape(acc.shape)
        for k in range(SIDE):
            for j in range(SIDE):
                own[j, k, :, cols] = acc[chip_at(pos, core, j, k, 1) * 2 + core].astype(BF)
                other[j, k, :, cols] = acc[chip_at(pos, 1 - core, j, k, 1) * 2 + 1 - core].astype(BF)
        states[:, cols] = jnp.dot(pick[...], x[:, cols], preferred_element_type=F32)


def load_kernel(src, out, sem):
    copy = pltpu.make_async_copy(src, out, sem)
    copy.start()
    copy.wait()


def load_weights(weights):
    return pl.pallas_call(
        load_kernel,
        out_shape=jax.ShapeDtypeStruct(weights.shape, weights.dtype),
        in_specs=[anym()],
        out_specs=vmem(),
        scratch_shapes=[pltpu.SemaphoreType.DMA],
        compiler_params=params(12),
        cost_estimate=pl.CostEstimate(flops=0, bytes_accessed=2 * weights.size, transcendentals=0),
    )(weights)


def feed_forward(pos, pieces, pieces_t, gain, gate_up, down, pick):
    width = gain.shape[1]
    units = down.shape[0]
    pages, count = pick.shape
    part = jax.ShapeDtypeStruct((SIDE, SIDE, pages, width), BF)
    return pl.pallas_call(
        ffn_kernel,
        out_shape=(part, part, jax.ShapeDtypeStruct((pages, width), F32)),
        in_specs=[smem()] + [anym()] * 8 + [vmem()] * 4,
        out_specs=(vmem(),) * 3,
        scratch_shapes=[
            pltpu.VMEM((count, 2 * SIDE * SIDE * HD), BF),
            pltpu.VMEM((count, width), BF),
            pltpu.VMEM((count, units), BF),
            pltpu.VMEM((count // pages, pages, 512), F32),
            pltpu.SemaphoreType.DMA((40,)),
        ],
        compiler_params=params(12),
        cost_estimate=pl.CostEstimate(
            flops=6 * count * width * units, bytes_accessed=6 * width * units, transcendentals=0
        ),
    )(pos, *pieces, *pieces_t, gain, gate_up, down, pick)


def on_device(
    tokens,
    page_lengths,
    page_group,
    page_report,
    attn_gain,
    w_query,
    w_keyval,
    w_out,
    doc_gain,
    ffn_gain,
    gate_up_weight,
    w_down,
):
    count, width = tokens.shape
    pages = page_lengths.shape[1]
    grp = lax.axis_index("grp")
    page = lax.axis_index("page")
    core = page % 2
    z = (page // 2) % SIDE
    x = page // (2 * SIDE)
    pos = jnp.stack([core, grp, x, z]).astype(jnp.int32)

    out_half = w_out.shape[1] // 2
    q_half = w_query.shape[1] // 2

    def out_cols(c):
        return lax.dynamic_slice_in_dim(w_out, c * out_half, out_half, 1)

    def qkv_cols(c):
        return jnp.concatenate(
            [
                lax.dynamic_slice_in_dim(w_query, c * q_half, q_half, 1),
                lax.dynamic_slice_in_dim(w_keyval, c * HD, HD, 1),
                lax.dynamic_slice_in_dim(w_keyval, (2 + c) * HD, HD, 1),
            ],
            axis=1,
        )

    def pair_up(mine, got):
        low = jnp.where(core == 0, mine, got)
        high = jnp.where(core == 0, got, mine)
        return jnp.concatenate([low, high], axis=0)

    wo_got = swap(out_cols(1 - core))
    w_query, w_keyval, wo_got = lax.optimization_barrier((w_query, w_keyval, wo_got))
    wo = pair_up(out_cols(core), wo_got)
    wq = pair_up(qkv_cols(core), swap(qkv_cols(1 - core)))
    wo_y = lax.dynamic_slice_in_dim(wo, grp * WY, WY, 1)
    tile = (out_half - SIDE * WY) // 2
    wo_r = wo[:, SIDE * WY :]
    wq = jnp.concatenate([wq, jnp.concatenate([wo_r[:, :tile], wo_r[:, tile:]], axis=0)], axis=1)

    tok_other = swap(tokens)
    len_other = swap(page_lengths)
    gain = attn_gain[None, :]
    x_own = norm_blocks(tokens, gain)
    x_other = norm_blocks(tok_other, gain)
    seg_own = page_index(page_lengths[0], count)
    seg_other = page_index(len_other[0], count)
    seg_col = jnp.concatenate([seg_own, seg_other])[:, None]
    seg_row = jnp.stack([seg_own, seg_other])[:, None, :]
    names = jnp.arange(pages, dtype=jnp.int32)[:, None]
    members = tuple((seg[None, :] == names).astype(BF) for seg in (seg_own, seg_other))
    lens = tuple(v[0][:, None].astype(F32) for v in (page_lengths, len_other))
    slots = 2 * SIDE * SIDE
    plane = slots * pages
    labels = page_group * REPORTS + page_report[:, None]
    head_gain = jnp.pad(doc_gain, (0, slots * HD - width))
    head_gain = lax.dynamic_slice_in_dim(head_gain, page * HD, HD)[None, :]
    pick = (
        jnp.arange(plane, dtype=jnp.int32)[None, :] == page * pages + jnp.arange(pages)[:, None]
    ).astype(BF)
    early = (seg_col, seg_row, members, lens, labels, head_gain, pick, pos, ffn_gain[None, :])

    line_y = jnp.stack([wo_y, move_a(wo_y, 1), move_a(wo_y, 2), move_a(wo_y, -1)])
    line_y, wq = lax.optimization_barrier((line_y, wq))
    square = (line_y, move_b(line_y, 1), move_b(line_y, 2), move_b(line_y, -1))
    q1, q3 = move_a(wq, 1), move_a(wq, -1)
    square, q1, q3 = lax.optimization_barrier((square, q1, q3))
    q1, q2, q3 = lax.optimization_barrier((q1, move_a(wq, 2), q3))
    wo_all = lax.all_gather(arrange(pos, square), "grp", axis=0, tiled=True)
    wo_all = wo_all.reshape(SIDE, -1, WY)
    low = jnp.stack([wq, q1])
    high = jnp.stack([q2, q3])
    up = [move_b(low, 1), move_b(high, 1)]
    down = [move_b(low, -1), move_b(high, -1)]
    up[0], x_own, x_other, early = lax.optimization_barrier((up[0], x_own, x_other, early))
    far = [move_b(up[0], 1), move_b(down[1], -1)]
    pieces = [low, high] + up + far + down
    seg_col, seg_row, members, lens, labels, head_gain, pick, pos, ffn_row = early

    part = qkv_first(pos, x_own, x_other, pieces[:4] + pieces[6:], QKV_COLS)
    att = qkv_last(pos, x_own, x_other, seg_col, seg_row, part, far)
    att_in = swap(att)
    st_own, st_other, pool_own, pool_other = page_out(
        pos, tokens, tok_other, att, att_in, members, lens, wo_all, pieces
    )

    def side_by_side(mine, got):
        left = jnp.where(core == 0, mine, got)
        right = jnp.where(core == 0, got, mine)
        return jnp.concatenate([left, right], axis=1)

    vectors = side_by_side(pool_own, swap(pool_other))
    token_states = side_by_side(st_own, swap(st_other))

    blocks = page_blocks(vectors, labels, slots)
    blocks = jnp.broadcast_to(blocks[None], (SIDE,) + blocks.shape).reshape(-1, pages, 2 * HD)
    gathered = lax.all_to_all(blocks, ("grp", "page"), split_axis=0, concat_axis=0, tiled=True)
    mixed = doc_attention(pos, gathered.reshape(-1, 2 * HD), head_gain, plane)

    line = jnp.stack([mixed, move_a(mixed, 1), move_a(mixed, 2), move_a(mixed, -1)])
    line, gate_up_weight = lax.optimization_barrier((line, gate_up_weight))
    gate_up_weight = load_weights(gate_up_weight)
    pieces = (line, move_b(line, 1), move_b(line, 2), move_b(line, -1))
    pieces_t = tuple(swap(v) for v in pieces)
    own, other, states = feed_forward(
        pos, pieces, pieces_t, ffn_row, gate_up_weight, w_down, pick
    )
    got = swap(other)

    def total(*terms):
        return sum(v.astype(F32) for v in terms)

    part = [total(own[j], got[j]).astype(BF) for j in range(SIDE)]
    part = total(part[0], *(move_a(part[j], j) for j in range(1, SIDE)))
    part = [part[k].astype(BF) if k else part[k] for k in range(SIDE)]
    summed = total(part[0], *(move_b(part[k], k) for k in range(1, SIDE)))
    page_embeddings = (states + summed).astype(BF)
    return (token_states, page_embeddings)


def solution(mesh):
    in_specs = (
        P(("grp", "page"), None),
        P(("grp", "page"), None),
        P(("grp", "page"), None),
        P(("grp", "page")),
        P(),
        P("page", None),
        P("page", None),
        P("page", None),
        P(),
        P(),
        P(None, None, "page"),
        P("page", None),
    )
    out_specs = (P(("grp", "page"), None), P(("grp", "page"), None))
    return jax.shard_map(
        on_device, mesh=mesh, in_specs=in_specs, out_specs=out_specs, check_vma=False
    )
```

```python
import functools
import math

import jax
import jax.numpy as jnp
from jax import lax
from jax.experimental import pallas as pl
from jax.experimental.pallas import tpu as pltpu
from jax.sharding import PartitionSpec as P

HD = 128
REPORTS = 16
SIDE = 4
WY = 384
BF = jnp.bfloat16
F32 = jnp.float32
MIB = 1 << 20


def vmem():
    return pl.BlockSpec(memory_space=pltpu.VMEM)


def smem():
    return pl.BlockSpec(memory_space=pltpu.SMEM)


def anym():
    return pl.BlockSpec(memory_space=pl.ANY)


def params(mib):
    return pltpu.CompilerParams(vmem_limit_bytes=mib * MIB)


def chip_perm(step):
    pairs = []
    for x in range(SIDE):
        for z in range(SIDE):
            for c in range(2):
                a, b, d = step(x, z, c)
                pairs.append(((x * SIDE + z) * 2 + c, ((a % SIDE) * SIDE + b % SIDE) * 2 + d))
    return pairs


def swap(v):
    return lax.ppermute(v, "page", chip_perm(lambda x, z, c: (x, z, 1 - c)))


def move_a(v, k):
    return lax.ppermute(
        v, "page", chip_perm(lambda x, z, c: (x + k, z, c) if c == 0 else (x, z + k, c))
    )


def move_b(v, k):
    return lax.ppermute(
        v, "page", chip_perm(lambda x, z, c: (x, z + k, c) if c == 0 else (x + k, z, c))
    )


def rms_scale(values, gain):
    wide = values.astype(F32)
    return wide * lax.rsqrt(jnp.mean(wide * wide, axis=-1, keepdims=True) + 1e-06) * gain


def page_index(lengths, count):
    ends = jnp.cumsum(lengths, dtype=jnp.int32)
    position = jnp.arange(count, dtype=jnp.int32)
    return jnp.sum((position[:, None] >= ends[None, :]).astype(jnp.int32), axis=1)


def chip_at(pos, core, j, k, sign):
    shift_x = jnp.where(core == 0, sign * j, sign * k)
    shift_z = jnp.where(core == 0, sign * k, sign * j)
    return lax.rem(pos[2] + SIDE + shift_x, SIDE) * SIDE + lax.rem(pos[3] + SIDE + shift_z, SIDE)


def run_copies(copies, sems):
    started = []
    for i, (src, dst) in enumerate(copies):
        copy = pltpu.make_async_copy(src, dst, sems.at[i])
        copy.start()
        started.append(copy)
    return started


QKV_COLS = 1152
BLOCK = 256


def norm_kernel(tok, gain, out, wide_ref):
    chunk = 32
    depth = tok.shape[1] // out.shape[0]

    @pl.loop(0, tok.shape[0] // chunk)
    def _(i):
        rows = pl.ds(pl.multiple_of(i * chunk, chunk), chunk)
        wide = tok[rows, :].astype(F32)
        scale = lax.rsqrt(jnp.mean(wide * wide, axis=1, keepdims=True) + 1e-06)
        wide_ref[...] = wide * scale * gain[...]
        for n in range(out.shape[0]):
            piece = wide_ref[:, n * depth : (n + 1) * depth]
            pad = jnp.zeros((chunk, BLOCK - depth), F32)
            out[n, rows, :] = jnp.concatenate([piece, pad], axis=1).astype(BF)


def norm_blocks(tok, gain):
    count, width = tok.shape
    chips = SIDE * SIDE
    return pl.pallas_call(
        norm_kernel,
        out_shape=jax.ShapeDtypeStruct((chips, count, BLOCK), BF),
        in_specs=[vmem()] * 2,
        out_specs=vmem(),
        scratch_shapes=[pltpu.VMEM((32, width), F32)],
        compiler_params=params(24),
        cost_estimate=pl.CostEstimate(flops=0, bytes_accessed=4 * count * width, transcendentals=0),
    )(tok, gain)


def qkv_load(pos, steps, pieces, xo, xt, w, x, sems):
    cols = w.shape[1]
    depth = pieces[0].shape[1]
    tokens = xo.shape[1]
    copies = []
    for n in range(2 * len(pieces)):
        piece = pieces[n // 2].at[n % 2, :, pl.ds(0, cols)]
        copies.append((piece, w.at[pl.ds(n * BLOCK, depth), :]))
    started = run_copies(copies, sems)
    for n in range(2 * len(pieces)):
        q = chip_at(pos, pos[0], n % SIDE, steps[n // SIDE], -1)
        x[0:tokens, n * BLOCK : (n + 1) * BLOCK] = xo[q]
        x[tokens : 2 * tokens, n * BLOCK : (n + 1) * BLOCK] = xt[q]
        w[n * BLOCK + depth : (n + 1) * BLOCK, :] = jnp.zeros((BLOCK - depth, cols), BF)
    for copy in started:
        copy.wait()


QKV_TILE = 384


def qkv_first_kernel(pos, xo, xt, *refs):
    *pieces, part, w, x, sems = refs
    qkv_load(pos, (0, 1, 3), pieces, xo, xt, w, x, sems)

    @pl.loop(0, part.shape[1] // QKV_TILE)
    def _(n):
        there = pl.ds(pl.multiple_of(n * QKV_TILE, 128), QKV_TILE)
        part[:, there] = jnp.dot(x[...], w[:, there], preferred_element_type=F32)


def qkv_last_kernel(pos, xo, xt, seg_col, seg_row, part, *refs):
    *pieces, out, w, x, qkv, sems = refs
    qkv_load(pos, (2,), pieces, xo, xt, w, x, sems)

    for lo in range(0, part.shape[1], BLOCK):
        there = slice(lo, min(lo + BLOCK, part.shape[1]))
        last = jnp.dot(x[...], w[:, there], preferred_element_type=F32)
        qkv[:, there] = (part[:, there] + last).astype(BF)

    heads = out.shape[1] // HD
    tokens = xo.shape[1]

    @pl.loop(0, 2)
    def _(b):
        rows = pl.ds(pl.multiple_of(b * tokens, tokens), tokens)
        same = seg_col[rows, :] == seg_row[b]
        keys = qkv[rows, heads * HD : (heads + 1) * HD]
        values = jnp.concatenate(
            [qkv[rows, (heads + 1) * HD : (heads + 2) * HD], jnp.ones((tokens, HD), BF)], axis=1
        )
        for h in range(heads):
            query = qkv[rows, h * HD : (h + 1) * HD]
            scores = lax.dot_general(
                query, keys, (((1,), (1,)), ((), ())), preferred_element_type=F32
            ) * (math.log2(math.e) / math.sqrt(HD))
            scores = jnp.where(same, scores, -1e30)
            top = jnp.max(scores, axis=1, keepdims=True)
            weights = jnp.exp2(scores - top).astype(BF)
            mixed = jnp.dot(weights, values, preferred_element_type=F32)
            out[rows, h * HD : (h + 1) * HD] = (mixed[:, 0:HD] / mixed[:, HD : 2 * HD]).astype(BF)


def qkv_first(pos, x_own, x_other, pieces, cols):
    tokens = x_own.shape[1]
    return pl.pallas_call(
        qkv_first_kernel,
        out_shape=jax.ShapeDtypeStruct((2 * tokens, cols), F32),
        in_specs=[smem()] + [vmem()] * 2 + [anym()] * 6,
        out_specs=vmem(),
        scratch_shapes=[
            pltpu.VMEM((12 * BLOCK, cols), BF),
            pltpu.VMEM((2 * tokens, 12 * BLOCK), BF),
            pltpu.SemaphoreType.DMA((12,)),
        ],
        compiler_params=params(40),
        cost_estimate=pl.CostEstimate(
            flops=4 * tokens * 12 * BLOCK * cols, bytes_accessed=24 * BLOCK * cols, transcendentals=0
        ),
    )(pos, x_own, x_other, *pieces)


def qkv_last(pos, x_own, x_other, seg_col, seg_row, part, pieces):
    tokens = x_own.shape[1]
    cols = part.shape[1]
    return pl.pallas_call(
        qkv_last_kernel,
        out_shape=jax.ShapeDtypeStruct((2 * tokens, cols - 2 * HD), BF),
        in_specs=[smem()] + [vmem()] * 5 + [anym()] * 2,
        out_specs=vmem(),
        scratch_shapes=[
            pltpu.VMEM((4 * BLOCK, cols), BF),
            pltpu.VMEM((2 * tokens, 4 * BLOCK), BF),
            pltpu.VMEM((2 * tokens, cols), BF),
            pltpu.SemaphoreType.DMA((4,)),
        ],
        compiler_params=params(40),
        cost_estimate=pl.CostEstimate(
            flops=4 * tokens * 8 * BLOCK * cols, bytes_accessed=24 * BLOCK * cols, transcendentals=0
        ),
    )(pos, x_own, x_other, seg_col, seg_row, part, *pieces)


def arrange_kernel(pos, t, b1, b2, b3, out):
    for k, piece in enumerate((t, b1, b2, b3)):
        for j in range(SIDE):
            out[chip_at(pos, pos[0], j, k, -1)] = piece[j]


def arrange(pos, pieces):
    n, rows, cols = pieces[0].shape
    return pl.pallas_call(
        arrange_kernel,
        out_shape=jax.ShapeDtypeStruct((SIDE * n, rows, cols), BF),
        in_specs=[smem()] + [vmem()] * 4,
        out_specs=vmem(),
        compiler_params=params(16),
        cost_estimate=pl.CostEstimate(
            flops=0, bytes_accessed=4 * SIDE * n * rows * cols, transcendentals=0
        ),
    )(pos, *pieces)


def out_kernel(
    pos, tok_own, tok_other, att, att_in, member, member_t, inv, inv_t, w_all, *refs
):
    pieces, refs = refs[: 2 * SIDE], refs[2 * SIDE :]
    st_own, st_other, pool_own, pool_other, w, rest, full, sems = refs
    core = pos[0]
    wy = w_all.shape[2]
    depth = pieces[0].shape[1] // 2
    tile = rest.shape[1] // 2
    chips = SIDE * SIDE
    copies = []
    rows = [
        pl.ds(pl.multiple_of(chip_at(pos, core, n % SIDE, n // SIDE, -1) * depth, 16), depth)
        for n in range(chips)
    ]
    for i in range(SIDE):
        copies.append((w_all.at[i], w.at[i]))
    for n in range(chips):
        for t in range(2):
            copies.append(
                (
                    pieces[n // 2].at[n % 2, pl.ds(t * depth, depth), pl.ds(QKV_COLS, tile)],
                    rest.at[rows[n], pl.ds(t * tile, tile)],
                )
            )
    started = run_copies(copies, sems)
    tokens = tok_own.shape[0]
    half = att.shape[1]
    mine = pl.ds(pl.multiple_of(core * half, 128), half)
    theirs = pl.ds(pl.multiple_of((1 - core) * half, 128), half)
    full[:, mine] = att[...]
    full[0:tokens, theirs] = att_in[tokens : 2 * tokens, :]
    full[tokens : 2 * tokens, theirs] = att_in[0:tokens, :]
    width = st_own.shape[1]

    def columns(lo, n, weight):
        cols = slice(lo, lo + n)
        there = pl.ds(pl.multiple_of(core * width + lo, 128), n)
        projected = jnp.dot(full[...], weight, preferred_element_type=F32)
        for first, tok, st, mem, ratio, pool in (
            (0, tok_own, st_own, member, inv, pool_own),
            (tokens, tok_other, st_other, member_t, inv_t, pool_other),
        ):
            states = (tok[:, there].astype(F32) + projected[first : first + tokens]).astype(BF)
            st[:, cols] = states
            pool[:, cols] = (
                jnp.dot(mem[...], states, preferred_element_type=F32) / ratio[...]
            ).astype(BF)

    for i in range(SIDE):
        started[i].wait()
        columns(i * wy, wy, w[i])
    for copy in started[SIDE:]:
        copy.wait()
    columns(SIDE * wy, 2 * tile, rest[...])


def page_out(pos, tok_own, tok_other, att, att_in, members, lens, w_all, pieces):
    tokens, width = tok_own.shape
    width = width // 2
    rows, wy = w_all.shape[1:]
    pages = members[0].shape[0]
    st = jax.ShapeDtypeStruct((tokens, width), BF)
    pool = jax.ShapeDtypeStruct((pages, width), BF)
    return pl.pallas_call(
        out_kernel,
        out_shape=(st, st, pool, pool),
        in_specs=[smem()] + [vmem()] * 8 + [anym()] * 9,
        out_specs=(vmem(),) * 4,
        scratch_shapes=[
            pltpu.VMEM((SIDE, rows, wy), BF),
            pltpu.VMEM((rows, width - SIDE * wy), BF),
            pltpu.VMEM((2 * tokens, rows), BF),
            pltpu.SemaphoreType.DMA((SIDE + 2 * SIDE * SIDE,)),
        ],
        compiler_params=params(40),
        cost_estimate=pl.CostEstimate(
            flops=2 * 2 * tokens * width * rows, bytes_accessed=2 * width * rows, transcendentals=0
        ),
    )(pos, tok_own, tok_other, att, att_in, *members, *lens, w_all, *pieces)


def block_kernel(vec, label, out):
    pages, width = vec.shape
    wide = vec[...].astype(F32)
    scale = lax.rsqrt(jnp.mean(wide * wide, axis=1, keepdims=True) + 1e-06)
    high = scale.astype(BF)
    low = (scale - high.astype(F32)).astype(BF)
    lane = lax.broadcasted_iota(jnp.int32, (pages, HD), 1)
    side = jnp.where(lane == 0, high.astype(F32), jnp.where(lane == 1, low.astype(F32), 0.0))
    side = jnp.where(lane == 2, label[...].astype(F32), side).astype(BF)
    for h in range(width // HD):
        out[h, :, 0:HD] = vec[:, h * HD : (h + 1) * HD]
        out[h, :, HD : 2 * HD] = side
    for h in range(width // HD, out.shape[0]):
        out[h] = jnp.zeros((pages, 2 * HD), BF)


def page_blocks(vectors, labels, slots):
    return pl.pallas_call(
        block_kernel,
        out_shape=jax.ShapeDtypeStruct((slots, vectors.shape[0], 2 * HD), BF),
        in_specs=[vmem()] * 2,
        out_specs=vmem(),
        compiler_params=params(16),
    )(vectors, labels)


def doc_kernel(pos, rows, gain, out, keys_ref):
    count = out.shape[0]
    every = rows.shape[0]
    start = pl.multiple_of(pos[1] * count, count)
    mine = pl.ds(start, count)
    side = rows[:, HD : 2 * HD].astype(F32)
    scale = side[:, 0:1] + side[:, 1:2]
    keys = (rows[:, 0:HD].astype(F32) * scale * gain[...]).astype(BF)
    keys_ref[...] = keys
    query = keys_ref[mine, :]
    pick = (lax.broadcasted_iota(jnp.int32, (8, HD), 1) == 2).astype(BF)
    label_row = lax.dot_general(
        pick, rows[:, HD : 2 * HD], (((1,), (1,)), ((), ())), preferred_element_type=F32
    )[0:1, :]
    label_col = rows[mine, HD : 2 * HD].astype(F32)[:, 2:3]
    scores = lax.dot_general(
        query, keys, (((1,), (1,)), ((), ())), preferred_element_type=F32
    ) * (math.log2(math.e) / HD)
    scores = jnp.where(label_col == label_row, scores, -1e30)
    top = jnp.max(scores, axis=1, keepdims=True)
    e = jnp.exp2(scores - top)
    weights = (e * (1.0 / jnp.sum(e, axis=1, keepdims=True))).astype(BF)
    context = jnp.dot(weights, keys, preferred_element_type=F32)
    out[...] = (rows[mine, 0:HD].astype(F32) + context).astype(BF)


def doc_attention(pos, rows, gain, count):
    return pl.pallas_call(
        doc_kernel,
        out_shape=jax.ShapeDtypeStruct((count, HD), BF),
        in_specs=[smem()] + [vmem()] * 2,
        out_specs=vmem(),
        scratch_shapes=[pltpu.VMEM((rows.shape[0], HD), BF)],
        compiler_params=params(24),
    )(pos, rows, gain)


def ffn_kernel(
    pos, t, b1, b2, b3, tt, c1, c2, c3, gain, wgu, wd, pick,
    own, other, states, x, mixed, hidden, acc, sems,
):
    core = pos[0]
    width = gain.shape[1]
    units = hidden.shape[1]
    half = units // 2
    copies = []
    for side, pieces in ((core, (t, b1, b2, b3)), (1 - core, (tt, c1, c2, c3))):
        for k, piece in enumerate(pieces):
            for j in range(SIDE):
                head = chip_at(pos, side, j, k, -1) * 2 + side
                copies.append((piece.at[j], x.at[:, pl.ds(pl.multiple_of(head * HD, HD), HD)]))
    for copy in run_copies(copies, sems):
        copy.wait()
    chunk = 32

    @pl.loop(0, x.shape[0] // chunk)
    def _(i):
        rows = pl.ds(pl.multiple_of(i * chunk, chunk), chunk)
        wide = x[rows, 0:width].astype(F32)
        scale = lax.rsqrt(jnp.mean(wide * wide, axis=1, keepdims=True) + 1e-06)
        mixed[rows, :] = (wide * scale * gain[...]).astype(BF)

    for n in range(2):
        cols = slice(n * half, (n + 1) * half)
        gate = jnp.dot(mixed[...], wgu[0, :, cols], preferred_element_type=F32)
        up = jnp.dot(mixed[...], wgu[1, :, cols], preferred_element_type=F32)
        hidden[:, cols] = (gate * jax.nn.sigmoid(gate) * up).astype(BF)
    tile = acc.shape[2]

    @pl.loop(0, width // tile)
    def _(n):
        cols = pl.ds(pl.multiple_of(n * tile, 128), tile)
        part = jnp.dot(hidden[...], wd[:, cols], preferred_element_type=F32)
        acc[...] = part.reshape(acc.shape)
        for k in range(SIDE):
            for j in range(SIDE):
                own[j, k, :, cols] = acc[chip_at(pos, core, j, k, 1) * 2 + core].astype(BF)
                other[j, k, :, cols] = acc[chip_at(pos, 1 - core, j, k, 1) * 2 + 1 - core].astype(BF)
        states[:, cols] = jnp.dot(pick[...], x[:, cols], preferred_element_type=F32)


def load_kernel(src, out, sem):
    copy = pltpu.make_async_copy(src, out, sem)
    copy.start()
    copy.wait()


def load_weights(weights):
    return pl.pallas_call(
        load_kernel,
        out_shape=jax.ShapeDtypeStruct(weights.shape, weights.dtype),
        in_specs=[anym()],
        out_specs=vmem(),
        scratch_shapes=[pltpu.SemaphoreType.DMA],
        compiler_params=params(12),
        cost_estimate=pl.CostEstimate(flops=0, bytes_accessed=2 * weights.size, transcendentals=0),
    )(weights)


def feed_forward(pos, pieces, pieces_t, gain, gate_up, down, pick):
    width = gain.shape[1]
    units = down.shape[0]
    pages, count = pick.shape
    part = jax.ShapeDtypeStruct((SIDE, SIDE, pages, width), BF)
    return pl.pallas_call(
        ffn_kernel,
        out_shape=(part, part, jax.ShapeDtypeStruct((pages, width), F32)),
        in_specs=[smem()] + [anym()] * 8 + [vmem()] * 4,
        out_specs=(vmem(),) * 3,
        scratch_shapes=[
            pltpu.VMEM((count, 2 * SIDE * SIDE * HD), BF),
            pltpu.VMEM((count, width), BF),
            pltpu.VMEM((count, units), BF),
            pltpu.VMEM((count // pages, pages, width // 2), F32),
            pltpu.SemaphoreType.DMA((40,)),
        ],
        compiler_params=params(20),
        cost_estimate=pl.CostEstimate(
            flops=6 * count * width * units, bytes_accessed=6 * width * units, transcendentals=0
        ),
    )(pos, *pieces, *pieces_t, gain, gate_up, down, pick)


def on_device(
    tokens,
    page_lengths,
    page_group,
    page_report,
    attn_gain,
    w_query,
    w_keyval,
    w_out,
    doc_gain,
    ffn_gain,
    gate_up_weight,
    w_down,
):
    count, width = tokens.shape
    pages = page_lengths.shape[1]
    grp = lax.axis_index("grp")
    page = lax.axis_index("page")
    core = page % 2
    z = (page // 2) % SIDE
    x = page // (2 * SIDE)
    pos = jnp.stack([core, grp, x, z]).astype(jnp.int32)

    out_half = w_out.shape[1] // 2
    q_half = w_query.shape[1] // 2

    def out_cols(c):
        return lax.dynamic_slice_in_dim(w_out, c * out_half, out_half, 1)

    def qkv_cols(c):
        return jnp.concatenate(
            [
                lax.dynamic_slice_in_dim(w_query, c * q_half, q_half, 1),
                lax.dynamic_slice_in_dim(w_keyval, c * HD, HD, 1),
                lax.dynamic_slice_in_dim(w_keyval, (2 + c) * HD, HD, 1),
            ],
            axis=1,
        )

    def pair_up(mine, got):
        low = jnp.where(core == 0, mine, got)
        high = jnp.where(core == 0, got, mine)
        return jnp.concatenate([low, high], axis=0)

    wo_got = swap(out_cols(1 - core))
    w_query, w_keyval, wo_got = lax.optimization_barrier((w_query, w_keyval, wo_got))
    wo = pair_up(out_cols(core), wo_got)
    wq = pair_up(qkv_cols(core), swap(qkv_cols(1 - core)))
    wo_y = lax.dynamic_slice_in_dim(wo, grp * WY, WY, 1)
    tile = (out_half - SIDE * WY) // 2
    wo_r = wo[:, SIDE * WY :]
    wq = jnp.concatenate([wq, jnp.concatenate([wo_r[:, :tile], wo_r[:, tile:]], axis=0)], axis=1)

    tok_other = swap(tokens)
    len_other = swap(page_lengths)
    gain = attn_gain[None, :]
    x_own = norm_blocks(tokens, gain)
    x_other = norm_blocks(tok_other, gain)
    seg_own = page_index(page_lengths[0], count)
    seg_other = page_index(len_other[0], count)
    seg_col = jnp.concatenate([seg_own, seg_other])[:, None]
    seg_row = jnp.stack([seg_own, seg_other])[:, None, :]
    names = jnp.arange(pages, dtype=jnp.int32)[:, None]
    members = tuple((seg[None, :] == names).astype(BF) for seg in (seg_own, seg_other))
    lens = tuple(v[0][:, None].astype(F32) for v in (page_lengths, len_other))
    slots = 2 * SIDE * SIDE
    plane = slots * pages
    labels = page_group * REPORTS + page_report[:, None]
    head_gain = jnp.pad(doc_gain, (0, slots * HD - width))
    head_gain = lax.dynamic_slice_in_dim(head_gain, page * HD, HD)[None, :]
    pick = (
        jnp.arange(plane, dtype=jnp.int32)[None, :] == page * pages + jnp.arange(pages)[:, None]
    ).astype(BF)
    early = (seg_col, seg_row, members, lens, labels, head_gain, pick, pos, ffn_gain[None, :])

    line_y = jnp.stack([wo_y, move_a(wo_y, 1), move_a(wo_y, 2), move_a(wo_y, -1)])
    line_y, wq = lax.optimization_barrier((line_y, wq))
    square = (line_y, move_b(line_y, 1), move_b(line_y, 2), move_b(line_y, -1))
    q1, q3 = move_a(wq, 1), move_a(wq, -1)
    square, q1, q3 = lax.optimization_barrier((square, q1, q3))
    q1, q2, q3 = lax.optimization_barrier((q1, move_a(wq, 2), q3))
    wo_all = lax.all_gather(arrange(pos, square), "grp", axis=0, tiled=True)
    wo_all = wo_all.reshape(SIDE, -1, WY)
    low = jnp.stack([wq, q1])
    high = jnp.stack([q2, q3])
    up = [move_b(low, 1), move_b(high, 1)]
    down = [move_b(low, -1), move_b(high, -1)]
    up[0], x_own, x_other, early = lax.optimization_barrier((up[0], x_own, x_other, early))
    far = [move_b(up[0], 1), move_b(down[1], -1)]
    pieces = [low, high] + up + far + down
    seg_col, seg_row, members, lens, labels, head_gain, pick, pos, ffn_row = early

    part = qkv_first(pos, x_own, x_other, pieces[:4] + pieces[6:], QKV_COLS)
    att = qkv_last(pos, x_own, x_other, seg_col, seg_row, part, far)
    att_in = swap(att)
    st_own, st_other, pool_own, pool_other = page_out(
        pos, tokens, tok_other, att, att_in, members, lens, wo_all, pieces
    )

    def side_by_side(mine, got):
        left = jnp.where(core == 0, mine, got)
        right = jnp.where(core == 0, got, mine)
        return jnp.concatenate([left, right], axis=1)

    vectors = side_by_side(pool_own, swap(pool_other))
    token_states = side_by_side(st_own, swap(st_other))

    blocks = page_blocks(vectors, labels, slots)
    blocks = jnp.broadcast_to(blocks[None], (SIDE,) + blocks.shape).reshape(-1, pages, 2 * HD)
    gathered = lax.all_to_all(blocks, ("grp", "page"), split_axis=0, concat_axis=0, tiled=True)
    gathered, gate_up_weight = lax.optimization_barrier((gathered, gate_up_weight))
    gate_up_weight = load_weights(gate_up_weight)
    mixed = doc_attention(pos, gathered.reshape(-1, 2 * HD), head_gain, plane)

    line = jnp.stack([mixed, move_a(mixed, 1), move_a(mixed, 2), move_a(mixed, -1)])
    line, gate_up_weight = lax.optimization_barrier((line, gate_up_weight))
    pieces = (line, move_b(line, 1), move_b(line, 2), move_b(line, -1))
    pieces_t = tuple(swap(v) for v in pieces)
    own, other, states = feed_forward(
        pos, pieces, pieces_t, ffn_row, gate_up_weight, w_down, pick
    )
    got = swap(other)

    def total(*terms):
        return sum(v.astype(F32) for v in terms)

    part = [total(own[j], got[j]).astype(BF) for j in range(SIDE)]
    part = total(part[0], *(move_a(part[j], j) for j in range(1, SIDE)))
    part = [part[k].astype(BF) if k else part[k] for k in range(SIDE)]
    summed = total(part[0], *(move_b(part[k], k) for k in range(1, SIDE)))
    page_embeddings = (states + summed).astype(BF)
    return (token_states, page_embeddings)


def solution(mesh):
    in_specs = (
        P(("grp", "page"), None),
        P(("grp", "page"), None),
        P(("grp", "page"), None),
        P(("grp", "page")),
        P(),
        P("page", None),
        P("page", None),
        P("page", None),
        P(),
        P(),
        P(None, None, "page"),
        P("page", None),
    )
    out_specs = (P(("grp", "page"), None), P(("grp", "page"), None))
    return jax.shard_map(
        on_device, mesh=mesh, in_specs=in_specs, out_specs=out_specs, check_vma=False
    )
```
